32 devices in a mesh: seq: 4 (over z), head: 8 (over y, x, core).
Axes of the slice: x: 2, y: 2, z: 4, core: 2. Of those that a mesh axis runs over, the one named last changes fastest.
Arguments:
- values: bfloat16 [4096, 8192], P('seq', 'head'), may hold values from -6 to 6
- gate_z: bfloat16 [4096, 8192], P('seq', 'head'), may hold values from -6 to 6
- b_keys: bfloat16 [4096, 8, 128], P('seq'), may hold values from -0.5 to 0.5
- c_queries: bfloat16 [4096, 8, 128], P('seq'), may hold values from -6 to 6
- log_decay: float32 [4096, 128], P('seq', 'head'), may hold values from -2.5 to 0
- level_weight: float32 [4096, 128, 7], P('seq', 'head'), may hold values from 0.2 to 2
- doc_start: int32 [64], replicated, may hold values 0 or 1
- norm_gain: float32 [8192], replicated, may hold values from 0.25 to 1.75
Outputs:
- normed: bfloat16 [4096, 8192], P(('seq', 'head'))
The draws below stay inside these ranges and needn't reach their ends.
All inputs are finite; a program needn't handle non-finite values.
Results may differ from the reference program's by a relative error of at most 0.0049.
Values may be sent and summed in bfloat16 or wider, within the bound.
No kernel may reach another device: no remote copies, remote signals or barrier semaphores. Data moves between devices by JAX's collectives and lax.ppermute only.
A program may use at most 192 MiB of HBM per device.

```python
import math
import jax
import jax.numpy as jnp
from jax import lax

MIXER_HEADS = 128
HEAD_DIM = 64
STATE = 128
GROUPS = 8
SPAN = 64
WINDOW_TOKENS = 4096
SPANS = 64
LEVELS = 7


def draw_log_decay(key, part):
    complete_keys = jax.random.split(key, 7)
    fast_share = 0.5
    fast_heads = jax.random.uniform(complete_keys[0], (MIXER_HEADS,)) < fast_share
    fast_rate = jnp.exp(jax.random.uniform(complete_keys[1], (MIXER_HEADS,), minval=math.log(1.0 / 50.0), maxval=math.log(1.0 / 30.0)))
    slow_rate = 0.3 * math.log(10.0) / WINDOW_TOKENS * jnp.exp(jax.random.uniform(complete_keys[2], (MIXER_HEADS,), minval=-0.3, maxval=0.3))
    default_rate = jnp.where(fast_heads, fast_rate, slow_rate)
    block_multiplier = jnp.exp(jax.random.uniform(complete_keys[3], (WINDOW_TOKENS // SPAN, 1, MIXER_HEADS), minval=-math.log(2.0), maxval=math.log(2.0)))
    block_multiplier = jnp.broadcast_to(block_multiplier, (WINDOW_TOKENS // SPAN, SPAN, MIXER_HEADS)).reshape(WINDOW_TOKENS, MIXER_HEADS)
    token_multiplier = jax.random.uniform(complete_keys[4], (WINDOW_TOKENS, MIXER_HEADS), minval=0.5, maxval=1.5)
    surge_position = jax.random.randint(complete_keys[5], (3,), 0, WINDOW_TOKENS)
    surge_length = jax.random.uniform(complete_keys[6], (3, MIXER_HEADS), minval=0.22, maxval=0.69)
    token_positions = jnp.arange(WINDOW_TOKENS)
    match_count = (token_positions[:, None] == surge_position[None, :]).astype(jnp.float32)
    surge_list = jnp.dot(match_count, surge_length)
    return (-(default_rate[None, :] * block_multiplier * token_multiplier) - surge_list).astype(jnp.float32)


def place_ends(array, key, low, top_value):
    spot = [jax.random.randint(jax.random.fold_in(key, axis), (), 0, length) for axis, length in enumerate(array.shape)]
    widest = array.shape.index(max(array.shape))
    beside = spot[:widest] + [(spot[widest] + 1) % array.shape[widest]] + spot[widest + 1:]
    return array.at[tuple(spot)].set(low).at[tuple(beside)].set(top_value)


def levels(own_key, shape, shards, smallest, largest):
    level, own = 1.0, jax.random.fold_in(own_key, 6)
    for position, parts in shards:
        draws = jnp.exp(jax.random.uniform(jax.random.fold_in(own, position), (parts,), jnp.float32, smallest / len(shards), largest / len(shards)))
        level = level * jnp.repeat(draws, shape[position] // parts).reshape([-1 if axis == position else 1 for axis in range(len(shape))])
    return level


def bell_draw(rng, dims, scale, limit, cuts=(), kind=jnp.bfloat16):
    values = jax.random.normal(rng, dims, jnp.float32) * scale
    if len(cuts) > 0:
        values = levels(rng, dims, cuts, -0.22, 0.18) * values
    return jnp.clip(values, min=-limit, max=limit).astype(kind)


def setup_inputs(seed: int = 0) -> dict:
    key_of = jax.random.split(jax.random.key(seed), 9)
    return {
        "values": bell_draw(key_of[0], (WINDOW_TOKENS, MIXER_HEADS * HEAD_DIM), 1.0, 6.0, ((0, 4), (1, 8))),
        "gate_z": bell_draw(key_of[1], (WINDOW_TOKENS, MIXER_HEADS * HEAD_DIM), 1.0, 6.0, ((0, 4), (1, 8))),
        "b_keys": bell_draw(key_of[2], (WINDOW_TOKENS, GROUPS, STATE), STATE ** -0.5, 0.5, ((0, 4),)),
        "c_queries": bell_draw(key_of[3], (WINDOW_TOKENS, GROUPS, STATE), 1.0, 6.0, ((0, 4),)),
        "log_decay": draw_log_decay(jax.random.fold_in(key_of[8], 71), 0),
        "level_weight": jnp.clip(jnp.exp(math.log(2.0) - 2.3025851 * jax.random.uniform(key_of[5], (WINDOW_TOKENS, MIXER_HEADS, LEVELS), jnp.float32) ** levels(key_of[5], (WINDOW_TOKENS, MIXER_HEADS, LEVELS), ((0, 4), (1, 8)), -0.2, 0.2)), 0.2, 2.0),
        "doc_start": place_ends((jax.random.randint(key_of[6], (SPANS,), 0, SPANS) < 2).astype(jnp.int32), jax.random.fold_in(key_of[6], 1), 0, 1),
        "norm_gain": jnp.clip(1.0 + 0.15 * jax.random.normal(key_of[7], (MIXER_HEADS * HEAD_DIM,), jnp.float32), 0.25, 1.75),
    }


def bit_count(operand, bit_width):
    result = jnp.zeros_like(operand)
    for offset in range(bit_width):
        result = result + (jnp.right_shift(operand, offset) > 0).astype(jnp.int32)
    return result

def reference(values, gate_z, b_keys, c_queries, log_decay, level_weight, doc_start, norm_gain):
    per_group = MIXER_HEADS // GROUPS
    highest = lax.Precision.HIGHEST
    counts = jnp.cumsum(doc_start).astype(jnp.int32)
    span_index = jnp.arange(SPANS, dtype=jnp.int32)
    span_level = bit_count(jnp.bitwise_xor(span_index[:, None], span_index[None, :]), LEVELS - 1)
    earlier = (span_index[None, :] < span_index[:, None]) & (counts[:, None] == counts[None, :])
    within = jnp.tril(jnp.ones((SPAN, SPAN), dtype=bool))
    level_masks = jnp.stack([span_level == level_index for level_index in range(1, LEVELS)]).astype(jnp.float32)

    def one_head(head_index):
        group_index = head_index // per_group
        key_rows = lax.dynamic_index_in_dim(b_keys, group_index, 1, keepdims=False).astype(jnp.float32).reshape(SPANS, SPAN, STATE)
        query_rows = lax.dynamic_index_in_dim(c_queries, group_index, 1, keepdims=False).astype(jnp.float32).reshape(SPANS, SPAN, STATE)
        inputs = lax.dynamic_slice_in_dim(values, head_index * HEAD_DIM, HEAD_DIM, 1).astype(jnp.float32).reshape(SPANS, SPAN, HEAD_DIM)
        decay_step = lax.dynamic_index_in_dim(log_decay, head_index, 1, keepdims=False)
        weights = lax.dynamic_index_in_dim(level_weight, head_index, 1, keepdims=False).reshape(SPANS, SPAN, LEVELS)
        decay_sum = jnp.cumsum(decay_step).reshape(SPANS, SPAN)
        span_start = decay_sum[:, 0] - decay_step.reshape(SPANS, SPAN)[:, 0]
        span_end = decay_sum[:, SPAN - 1]
        scores = jnp.einsum('ctn,csn->cts', query_rows, key_rows, precision=highest)
        log_gap = jnp.where(within[None], decay_sum[:, :, None] - decay_sum[:, None, :], -jnp.inf)
        masked = scores * jnp.exp(log_gap) * weights[:, :, 0][:, :, None]
        result = jnp.einsum('cts,csp->ctp', masked, inputs, precision=highest)
        key_scale = jnp.exp(span_end[:, None] - decay_sum)
        states = jnp.einsum('csn,csp->cnp', key_rows * key_scale[:, :, None], inputs, precision=highest)
        carry = jnp.exp(jnp.where(earlier, span_start[:, None] - span_end[None, :], -jnp.inf))
        incoming = jnp.einsum('lij,jnp->linp', level_masks * carry[None], states, precision=highest)
        projected = jnp.einsum('itn,linp->itlp', query_rows, incoming, precision=highest)
        far_coef = weights[:, :, 1:] * jnp.exp(decay_sum - span_start[:, None])[:, :, None]
        result = result + jnp.einsum('itl,itlp->itp', far_coef, projected, precision=highest)
        return result.reshape(WINDOW_TOKENS, HEAD_DIM)
    mixer = lax.map(one_head, jnp.arange(MIXER_HEADS, dtype=jnp.int32))
    mixer = jnp.transpose(mixer, (1, 0, 2)).reshape(WINDOW_TOKENS, MIXER_HEADS * HEAD_DIM).astype(jnp.bfloat16)
    gated = mixer.astype(jnp.float32) * jax.nn.silu(gate_z.astype(jnp.float32))
    grouped = gated.reshape(WINDOW_TOKENS, GROUPS, MIXER_HEADS * HEAD_DIM // GROUPS)
    inverse_rms = lax.rsqrt(lax.optimization_barrier(jnp.mean(grouped * grouped, axis=2, keepdims=True)) + 1e-05)
    return ((grouped * inverse_rms).reshape(WINDOW_TOKENS, MIXER_HEADS * HEAD_DIM) * norm_gain[None, :]).astype(jnp.bfloat16)
```

```python
import functools

import jax
import jax.numpy as jnp
from jax import lax
from jax.experimental import pallas as pl
from jax.experimental.pallas import tpu as pltpu
from jax.sharding import PartitionSpec as P

MIXER_HEADS = 128
GROUPS = 8
SPAN = 64
TILE = 2 * SPAN
LANES = 128
SUBLANES = 8
NEVER = -1e30
HIGHEST = lax.Precision.HIGHEST
MIB = 2**20


def dot(left, right, contract=((1,), (0,)), precision=None):
    return lax.dot_general(
        left, right, (contract, ((), ())), precision=precision, preferred_element_type=jnp.float32
    )


def iota(shape, axis):
    return lax.broadcasted_iota(jnp.int32, shape, axis)


def halves(coef):
    high = coef.astype(jnp.bfloat16)
    low = (coef - high.astype(jnp.float32)).astype(jnp.bfloat16)
    return jnp.concatenate([high, low], axis=1)


def spread(first, width, head_dim):
    row = jnp.bitwise_and(iota((2 * LANES, width), 0), LANES - 1)
    head = jnp.right_shift(iota((2 * LANES, width), 1), head_dim.bit_length() - 1)
    return jnp.where(row == head + first, 1.0, 0.0).astype(jnp.bfloat16)


def head_row(column, width, head_dim):
    shape = (column.shape[0], width)
    head = jnp.right_shift(iota(shape, 1), head_dim.bit_length() - 1)
    return jnp.sum(jnp.where(head == iota(shape, 0), column, 0.0), axis=0, keepdims=True)


def stack_rows(pieces):
    rows = sum(piece.shape[0] for piece in pieces)
    if rows < LANES:
        pieces = pieces + [jnp.zeros((LANES - rows, LANES), jnp.float32)]
    return jnp.transpose(jnp.concatenate(pieces, axis=0))


def state_kernel(head_dim, docs, decay, keys, inputs, state, message, through):
    heads, tokens = decay.shape
    width = inputs.shape[1]
    tiles = tokens // TILE
    first = lax.axis_index("seq") * (tokens // SPAN)
    lane = iota((heads, TILE), 1)
    later = jnp.where(iota((TILE, TILE), 0) > iota((TILE, TILE), 1), 1.0, 0.0)
    stacked = jnp.concatenate([decay[:, b * TILE : (b + 1) * TILE] for b in range(tiles)], axis=0)
    suffix = dot(stacked, later, precision=HIGHEST)
    totals = jnp.sum(stacked, axis=1, keepdims=True)
    after = jnp.zeros((heads, 1), jnp.float32)
    closed = jnp.float32(0.0)
    rows = [None] * tiles
    for b in reversed(range(tiles)):
        second = NEVER * docs[first + 2 * b + 1].astype(jnp.float32)
        shut = jnp.where(lane < SPAN, closed + second, closed)
        rows[b] = jnp.exp(suffix[b * heads : (b + 1) * heads] + after + shut)
        closed = closed + second + NEVER * docs[first + 2 * b].astype(jnp.float32)
        after = after + totals[b * heads : (b + 1) * heads]
    columns = stack_rows(rows)
    owner = jnp.right_shift(iota((TILE, LANES), 1), heads.bit_length() - 1)
    shape = (2 * LANES, width)
    same = jnp.bitwise_and(iota(shape, 0), heads - 1) == jnp.right_shift(
        iota(shape, 1), head_dim.bit_length() - 1
    )
    one_hot = jnp.where(same, 1.0, 0.0).astype(jnp.bfloat16)
    total = jnp.zeros((keys.shape[1], width), jnp.float32)
    for b in range(tiles):
        scale = dot(halves(jnp.where(owner == b, columns, 0.0)), one_hot)
        piece = inputs[b * TILE : (b + 1) * TILE, :].astype(jnp.float32) * scale
        total += dot(
            keys[b * TILE : (b + 1) * TILE, :], piece.astype(jnp.bfloat16), ((0,), (0,))
        )
    state[...] = total
    message[...] = total.astype(jnp.bfloat16)
    row = head_row(jnp.exp(after + closed), width, head_dim)
    through[...] = jnp.broadcast_to(row, through.shape)


def local_kernel(
    head_dim, far, docs, decay, weight, inputs, queries, keys, out, coefs, slots, run, hot, now
):
    heads = decay.shape[0]
    width = inputs.shape[1]
    near = slots.shape[0]
    tile = pl.program_id(0)
    first = lax.axis_index("seq") * (pl.num_programs(0) * (TILE // SPAN)) + 2 * tile
    lane = iota((heads, TILE), 1)
    early = iota((TILE, TILE), 1) < SPAN

    @pl.when(tile == 0)
    def _():
        run[...] = jnp.zeros_like(run)
        for index in range(near + 1):
            hot[index] = spread((2 + index) * heads, width, head_dim)

    shut_first = NEVER * docs[first].astype(jnp.float32)
    shut_second = NEVER * docs[first + 1].astype(jnp.float32)
    upto = jnp.where(iota((TILE, TILE), 0) <= iota((TILE, TILE), 1), 1.0, 0.0)
    sums = dot(decay[...], upto, precision=HIGHEST)
    last = jnp.broadcast_to(sums[:, TILE - 1 :], sums.shape)
    total = last + (shut_first + shut_second)
    opened = sums + jnp.where(lane < SPAN, shut_first, shut_first + shut_second)
    own = sums + jnp.log(weight[0])
    beside = jnp.where(lane < SPAN, own, sums + jnp.log(weight[1]) + shut_second)
    since = [
        jnp.where(jnp.bitwise_and(tile, 2**k - 1) == 0, 0.0, run[k]) for k in range(near)
    ] + [run[near]]
    rows = [own, beside]
    rows += [jnp.exp(opened + since[k]) * weight[2 + k] for k in range(near)]
    rows += [jnp.exp(last - sums + jnp.where(lane < SPAN, shut_second, 0.0))]
    rows += [jnp.exp(opened + since[near]) * weight[2 + near + m] for m in range(far)]
    for k in range(near + 1):
        run[k] = since[k] + total
    columns = stack_rows(rows)
    terms = halves(columns)
    coefs[...] = terms

    span_queries = queries[...]
    scores = dot(span_queries, keys[...], ((1,), (1,)))
    causal = iota((TILE, TILE), 0) >= iota((TILE, TILE), 1)
    per_tile = LANES // head_dim
    lane_head = jnp.right_shift(iota((TILE, LANES), 1), head_dim.bit_length() - 1)
    for part in range(width // LANES):
        block = inputs[:, part * LANES : (part + 1) * LANES]
        left, right = [], []
        for inner in range(per_tile):
            head = part * per_tile + inner
            gap = jnp.where(
                early,
                jnp.broadcast_to(columns[:, heads + head : heads + head + 1], (TILE, TILE)),
                jnp.broadcast_to(columns[:, head : head + 1], (TILE, TILE)),
            )
            gap = jnp.where(causal, gap - sums[head : head + 1, :], NEVER)
            left.append((jnp.exp(gap) * scores).astype(jnp.bfloat16))
            right.append(jnp.where(lane_head == inner, block, jnp.zeros_like(block)))
        out[:, part * LANES : (part + 1) * LANES] = dot(
            jnp.concatenate(left, axis=1), jnp.concatenate(right, axis=0)
        )
    for k in range(near):

        @pl.when(jnp.bitwise_and(jnp.right_shift(tile, k), 1) == 1)
        def _(k=k):
            out[...] += dot(terms, hot[k]) * dot(span_queries, slots[k].astype(jnp.bfloat16))

    scaled = (inputs[...].astype(jnp.float32) * dot(terms, hot[near])).astype(jnp.bfloat16)
    now[...] = dot(keys[...], scaled, ((0,), (0,)))
    for k in range(near):
        ready = jnp.bitwise_and(tile, 2**k - 1) == 2**k - 1
        full = jnp.bitwise_and(jnp.right_shift(tile, k), 1) == 1

        @pl.when(jnp.logical_and(ready, full))
        def _(k=k):
            row = head_row(jnp.exp(since[k] + total)[:, :1], width, head_dim)
            now[...] += slots[k] * row

        @pl.when(jnp.logical_and(ready, jnp.logical_not(full)))
        def _(k=k):
            slots[k] = now[...]


def gate_kernel(head_dim, heads, first, me, local, coefs, queries, states, gate, *rest):
    outs, hot = rest[:-1], rest[-1]
    step = pl.program_id(0)
    far, _, width = states.shape

    @pl.when(step == 0)
    def _():
        for m in range(far):
            hot[m] = spread(first + m * heads, width, head_dim)

    total = local[...]
    for m in range(far):
        total += dot(coefs[...], hot[m]) * dot(queries[...], states[m])
    opened = gate[...].astype(jnp.float32)
    gated = (total * (0.5 * opened) * (1.0 + jnp.tanh(0.5 * opened))).astype(jnp.bfloat16)
    if len(outs) == 1:
        outs[0][0] = gated
        return
    for index, out in enumerate(outs):

        @pl.when(step == index)
        def _(out=out):
            out[...] = gated


def norm_kernel(sources, me, gain, *rest):
    out = rest[-1]
    step = pl.program_id(0)

    def write(blocks):
        blocks = [block.astype(jnp.float32) for block in blocks]
        count = sum(block.shape[1] for block in blocks)
        square = sum(jnp.sum(block * block, axis=1, keepdims=True) for block in blocks)
        scale = lax.rsqrt(square / count + 1e-05)
        at = 0
        for block in blocks:
            end = at + block.shape[1]
            out[:, at:end] = (block * scale * gain[:, at:end]).astype(out.dtype)
            at = end

    if sources is None:
        parts = rest[:-1]
        write([part[index] for index in range(parts[0].shape[0]) for part in parts])
        return
    for index, places in enumerate(sources):

        @pl.when(step == index)
        def _(places=places):
            write([rest[place][...] for place in places])


def params(limit):
    return pltpu.CompilerParams(vmem_limit_bytes=limit * MIB)


def body(values, gate_z, b_keys, c_queries, log_decay, level_weight, doc_start, norm_gain):
    tokens, width = values.shape
    heads_here = log_decay.shape[1]
    head_dim = width // heads_here
    state_size = b_keys.shape[2]
    tiles = tokens // TILE
    near = tiles.bit_length() - 1
    seq_count = lax.axis_size("seq")
    far = seq_count.bit_length() - 1
    head_count = lax.axis_size("head")
    head_index = lax.axis_index("head")
    group_index = head_index * heads_here // (MIXER_HEADS // GROUPS)
    key_rows = lax.dynamic_index_in_dim(b_keys, group_index, 1, keepdims=False)
    query_rows = lax.dynamic_index_in_dim(c_queries, group_index, 1, keepdims=False)
    decay = jnp.transpose(log_decay)
    weight = jnp.transpose(level_weight, (2, 1, 0))
    heads = SUBLANES
    if heads_here < heads:
        short = heads - heads_here
        decay = jnp.pad(decay, ((0, short), (0, 0)))
        weight = jnp.pad(weight, ((0, 0), (0, short), (0, 0)), constant_values=1.0)
    chunks = max(1, heads_here // heads)
    part = width // chunks
    levels = weight.shape[0]
    smem = pl.BlockSpec(memory_space=pltpu.SMEM)

    def state_call(c):
        return pl.pallas_call(
            functools.partial(state_kernel, head_dim),
            grid=(1,),
            in_specs=[
                smem,
                pl.BlockSpec((heads, tokens), lambda i: (c, 0)),
                pl.BlockSpec((tokens, state_size), lambda i: (0, 0)),
                pl.BlockSpec((tokens, part), lambda i: (0, c)),
            ],
            out_specs=[
                pl.BlockSpec((state_size, part), lambda i: (0, 0)),
                pl.BlockSpec((state_size, part), lambda i: (0, 0)),
                pl.BlockSpec((SUBLANES, part), lambda i: (0, 0)),
            ],
            out_shape=[
                jax.ShapeDtypeStruct((state_size, part), jnp.float32),
                jax.ShapeDtypeStruct((state_size, part), jnp.bfloat16),
                jax.ShapeDtypeStruct((SUBLANES, part), jnp.float32),
            ],
            compiler_params=params(16),
            cost_estimate=pl.CostEstimate(
                flops=4 * tokens * state_size * part, bytes_accessed=3 * tokens * part, transcendentals=0
            ),
            name="block_state",
        )(doc_start, decay, key_rows, values)

    def local_call(c):
        return pl.pallas_call(
            functools.partial(local_kernel, head_dim, far),
            grid=(tiles,),
            in_specs=[
                smem,
                pl.BlockSpec((heads, TILE), lambda i: (c, i)),
                pl.BlockSpec((levels, heads, TILE), lambda i: (0, c, i)),
                pl.BlockSpec((TILE, part), lambda i: (i, c)),
                pl.BlockSpec((TILE, state_size), lambda i: (i, 0)),
                pl.BlockSpec((TILE, state_size), lambda i: (i, 0)),
            ],
            out_specs=[
                pl.BlockSpec((TILE, part), lambda i: (i, 0)),
                pl.BlockSpec((TILE, 2 * LANES), lambda i: (i, 0)),
            ],
            out_shape=[
                jax.ShapeDtypeStruct((tokens, part), jnp.float32),
                jax.ShapeDtypeStruct((tokens, 2 * LANES), jnp.bfloat16),
            ],
            scratch_shapes=[
                pltpu.VMEM((near, state_size, part), jnp.float32),
                pltpu.VMEM((near + 1, heads, TILE), jnp.float32),
                pltpu.VMEM((near + 1, 2 * LANES, part), jnp.bfloat16),
                pltpu.VMEM((state_size, part), jnp.float32),
            ],
            compiler_params=params(16),
            cost_estimate=pl.CostEstimate(
                flops=16 * tokens * state_size * part, bytes_accessed=12 * tokens * part, transcendentals=0
            ),
            name="local_mixer",
        )(doc_start, decay, weight, values, query_rows, key_rows)

    rows = tokens // head_count
    direct = head_count == GROUPS
    me = jnp.reshape(head_index, (1,)).astype(jnp.int32)

    def gate_call(c, local, coefs, states):
        if direct:
            place = lambda i, s: jnp.bitwise_xor(i, s[0])
            out_specs = [pl.BlockSpec((rows, part), lambda i, s: (0, 0))] * head_count
            out_shape = [jax.ShapeDtypeStruct((rows, part), jnp.bfloat16)] * head_count
        else:
            place = lambda i, s: i
            out_specs = [pl.BlockSpec((1, rows, part), lambda i, s: (i, 0, 0))]
            out_shape = [jax.ShapeDtypeStruct((head_count, rows, part), jnp.bfloat16)]
        return pl.pallas_call(
            functools.partial(gate_kernel, head_dim, heads, (near + 3) * heads),
            grid_spec=pltpu.PrefetchScalarGridSpec(
                num_scalar_prefetch=1,
                grid=(head_count,),
                in_specs=[
                    pl.BlockSpec((rows, part), lambda i, s: (place(i, s), 0)),
                    pl.BlockSpec((rows, 2 * LANES), lambda i, s: (place(i, s), 0)),
                    pl.BlockSpec((rows, state_size), lambda i, s: (place(i, s), 0)),
                    pl.BlockSpec((far, state_size, part), lambda i, s: (0, 0, 0)),
                    pl.BlockSpec((rows, part), lambda i, s: (place(i, s), c)),
                ],
                out_specs=out_specs,
                scratch_shapes=[pltpu.VMEM((far, 2 * LANES, part), jnp.bfloat16)],
            ),
            out_shape=out_shape,
            compiler_params=params(16),
            cost_estimate=pl.CostEstimate(
                flops=4 * tokens * state_size * part, bytes_accessed=8 * tokens * part, transcendentals=0
            ),
            name="far_and_gate",
        )(me, local, coefs, query_rows, states, gate_z)

    owns, throughs, messages = zip(*[(s, t[:1], m) for s, m, t in map(state_call, range(chunks))])
    owns = list(owns)
    carried = [[None] * far for _ in range(chunks)]
    for bit in range(far):
        size = 2**bit
        for c in range(chunks):
            moving = messages[c] if bit == 0 else owns[c].astype(jnp.bfloat16)
            arrived = None
            for hop in range(1, size + 1):
                source = [base + size + hop - 2 for base in range(0, seq_count, 2 * size)]
                got = lax.ppermute(moving, "seq", [(s, s + 1) for s in source])
                arrived = got if arrived is None else arrived + got
                passed = got.astype(jnp.float32) * throughs[c]
                moving = passed.astype(jnp.bfloat16)
            carried[c][bit] = arrived
            owns[c] = owns[c] + passed
    locals_ = [local_call(c) for c in range(chunks)]

    pieces = []
    for c in range(chunks):
        local, coefs = locals_[c]
        out = gate_call(c, local, coefs, jnp.stack(carried[c]))
        if direct:
            got = [out[0]] + [None] * (head_count - 1)
            for apart in sorted(range(1, head_count), key=lambda k: -k.bit_count() * 8 - k):
                pairs = [(source, source ^ apart) for source in range(head_count)]
                got[apart] = lax.ppermute(out[apart], "head", pairs)
            pieces.append(got)
        else:
            pieces.append(lax.all_to_all(out[0], "head", split_axis=0, concat_axis=0))

    gain = jnp.reshape(norm_gain, (1, -1))
    group_width = width * head_count // GROUPS
    if direct:
        flat = [piece for got in pieces for piece in got]
        sources = [[c * head_count + k for c in range(chunks)] for k in range(head_count)]
        column = lambda i, s: (0, jnp.bitwise_xor(i, s[0]))
        in_specs = [pl.BlockSpec((rows, part), lambda i, s: (0, 0))] * len(flat)
    else:
        flat = pieces
        sources = None
        per_group = max(1, group_width // width)
        column = lambda i, s: (0, i)
        in_specs = [pl.BlockSpec((per_group, rows, part), lambda i, s: (i, 0, 0))] * len(flat)
    return pl.pallas_call(
        functools.partial(norm_kernel, sources),
        grid_spec=pltpu.PrefetchScalarGridSpec(
            num_scalar_prefetch=1,
            grid=(GROUPS,),
            in_specs=[pl.BlockSpec((1, group_width), column)] + in_specs,
            out_specs=pl.BlockSpec((rows, group_width), column),
        ),
        out_shape=jax.ShapeDtypeStruct((rows, width * head_count), jnp.bfloat16),
        compiler_params=params(16),
        cost_estimate=pl.CostEstimate(
            flops=8 * tokens * width, bytes_accessed=4 * tokens * width, transcendentals=0
        ),
        name="norm_rows",
    )(me, gain, *flat)


def solution(mesh):
    in_specs = (
        P("seq", "head"),
        P("seq", "head"),
        P("seq", None, None),
        P("seq", None, None),
        P("seq", "head"),
        P("seq", "head", None),
        P(),
        P(),
    )
    out_specs = P(("seq", "head"), None)
    return jax.shard_map(body, mesh=mesh, in_specs=in_specs, out_specs=out_specs, check_vma=False)
```

```python
import functools

import jax
import jax.numpy as jnp
from jax import lax
from jax.experimental import pallas as pl
from jax.experimental.pallas import tpu as pltpu
from jax.sharding import PartitionSpec as P

MIXER_HEADS = 128
GROUPS = 8
SPAN = 64
TILE = 2 * SPAN
LANES = 128
SUBLANES = 8
NEVER = -1e30
HIGHEST = lax.Precision.HIGHEST
MIB = 2**20


def dot(left, right, contract=((1,), (0,)), precision=None):
    return lax.dot_general(
        left, right, (contract, ((), ())), precision=precision, preferred_element_type=jnp.float32
    )


def iota(shape, axis):
    return lax.broadcasted_iota(jnp.int32, shape, axis)


def halves(coef):
    high = coef.astype(jnp.bfloat16)
    low = (coef - high.astype(jnp.float32)).astype(jnp.bfloat16)
    return jnp.concatenate([high, low], axis=1)


def spread(first, width, head_dim):
    row = jnp.bitwise_and(iota((2 * LANES, width), 0), LANES - 1)
    head = jnp.right_shift(iota((2 * LANES, width), 1), head_dim.bit_length() - 1)
    return jnp.where(row == head + first, 1.0, 0.0).astype(jnp.bfloat16)


def head_row(column, width, head_dim):
    shape = (column.shape[0], width)
    head = jnp.right_shift(iota(shape, 1), head_dim.bit_length() - 1)
    return jnp.sum(jnp.where(head == iota(shape, 0), column, 0.0), axis=0, keepdims=True)


def stack_rows(pieces):
    rows = sum(piece.shape[0] for piece in pieces)
    if rows < LANES:
        pieces = pieces + [jnp.zeros((LANES - rows, LANES), jnp.float32)]
    return jnp.transpose(jnp.concatenate(pieces, axis=0))


def tile_rows(decay):
    tiles = decay.shape[1] // TILE
    return jnp.concatenate([decay[:, b * TILE : (b + 1) * TILE] for b in range(tiles)], axis=0)


def resets(docs, tiles):
    first = lax.axis_index("seq") * (tiles * (TILE // SPAN))
    shut = [NEVER * docs[first + s].astype(jnp.float32) for s in range(tiles * (TILE // SPAN))]
    return [shut[2 * b : 2 * b + 2] for b in range(tiles)]


def state_kernel(
    head_dim, column, pieces, docs, decay, keys, values, state, message, through, inputs, arrived
):
    heads, tokens = decay.shape
    width = inputs.shape[1]
    tiles = tokens // TILE
    rows = tokens // pieces
    copies = [
        pltpu.make_async_copy(
            values.at[pl.ds(i * rows, rows), pl.ds(column, width)],
            inputs.at[pl.ds(i * rows, rows), :],
            arrived.at[i],
        )
        for i in range(pieces)
    ]
    for copy in copies:
        copy.start()
    shut = resets(docs, tiles)
    lane = iota((heads, TILE), 1)
    later = jnp.where(iota((TILE, TILE), 0) > iota((TILE, TILE), 1), 1.0, 0.0)
    stacked = tile_rows(decay)
    suffix = dot(stacked, later, precision=HIGHEST)
    totals = jnp.sum(stacked, axis=1, keepdims=True)
    after = jnp.zeros((heads, 1), jnp.float32)
    closed = jnp.float32(0.0)
    scales = [None] * tiles
    for b in reversed(range(tiles)):
        ends = jnp.where(lane < SPAN, closed + shut[b][1], closed)
        scales[b] = jnp.exp(suffix[b * heads : (b + 1) * heads] + after + ends)
        closed = closed + shut[b][1] + shut[b][0]
        after = after + totals[b * heads : (b + 1) * heads]
    terms = halves(stack_rows(scales))
    row = head_row(jnp.exp(after + closed), width, head_dim)
    through[...] = jnp.broadcast_to(row, through.shape)
    owner = jnp.right_shift(
        jnp.bitwise_and(iota((1, 2 * LANES), 1), LANES - 1), heads.bit_length() - 1
    )
    shape = (2 * LANES, width)
    same = jnp.bitwise_and(iota(shape, 0), heads - 1) == jnp.right_shift(
        iota(shape, 1), head_dim.bit_length() - 1
    )
    one_hot = jnp.where(same, 1.0, 0.0).astype(jnp.bfloat16)
    chosen = [
        terms * jnp.where(owner == b, 1.0, 0.0).astype(jnp.bfloat16) for b in range(tiles)
    ]
    total = jnp.zeros(state.shape, jnp.float32)
    for i in range(pieces):
        span = tiles // pieces
        scale = dot(jnp.concatenate(chosen[i * span : (i + 1) * span], axis=0), one_hot)
        copies[i].wait()
        scaled = inputs[i * rows : (i + 1) * rows, :].astype(jnp.float32) * scale
        total += dot(
            keys[i * rows : (i + 1) * rows, :], scaled.astype(jnp.bfloat16), ((0,), (0,))
        )
    state[...] = total
    message[...] = total.astype(jnp.bfloat16)


def local_kernel(
    head_dim, column, far, docs, decay, weight, values, queries, keys, follow, out, coefs
):
    del follow
    heads, tokens = decay.shape
    width = out.shape[1]
    tiles = tokens // TILE
    near = tiles.bit_length() - 1
    shut = resets(docs, tiles)
    lane = iota((heads, TILE), 1)
    upto = jnp.where(iota((TILE, TILE), 0) <= iota((TILE, TILE), 1), 1.0, 0.0)
    all_sums = dot(tile_rows(decay[...]), upto, precision=HIGHEST)
    causal = iota((TILE, TILE), 0) >= iota((TILE, TILE), 1)
    per_tile = LANES // head_dim
    lane_head = jnp.right_shift(iota((TILE, LANES), 1), head_dim.bit_length() - 1)
    shape = (LANES, heads * TILE)
    row, col = iota(shape, 0), iota(shape, 1)
    group = jnp.right_shift(row, heads.bit_length() - 1)
    fits = jnp.bitwise_and(row, heads - 1) == jnp.right_shift(col, TILE.bit_length() - 1)
    older = jnp.bitwise_and(col, TILE - 1) < SPAN
    low, high = jnp.where(older, 3, 0), jnp.where(older, 6, 3)
    place = fits & (group >= low) & (group < high)
    place = jnp.where(place, 1.0, 0.0).astype(jnp.bfloat16)
    hot = [spread((6 + i) * heads, width, head_dim) for i in range(near + 1)]

    totals, slots = [], [None] * near
    for b in range(tiles):
        tokens_here = slice(b * TILE, (b + 1) * TILE)
        sums = all_sums[b * heads : (b + 1) * heads]
        scale = [weight[level, :, tokens_here] for level in range(weight.shape[0])]
        last = jnp.broadcast_to(sums[:, TILE - 1 :], sums.shape)
        opened = sums + jnp.where(lane < SPAN, shut[b][0], shut[b][0] + shut[b][1])
        own = sums + jnp.log(scale[0])
        beside = jnp.where(lane < SPAN, own, sums + jnp.log(scale[1]) + shut[b][1])
        rows = []
        for value in (own, beside):
            for _ in range(3):
                term = value.astype(jnp.bfloat16).astype(jnp.float32)
                rows.append(term)
                value = value - term
        levels = [k for k in range(near) if (b >> k) & 1]
        for k in range(near):
            if k in levels:
                since = sum(totals[(b >> k) << k : b], jnp.zeros_like(sums))
                rows.append(jnp.exp(opened + since) * scale[2 + k])
            else:
                rows.append(jnp.zeros_like(sums))
        rows.append(jnp.exp(last - sums + jnp.where(lane < SPAN, shut[b][1], 0.0)))
        since = sum(totals, jnp.zeros_like(sums))
        rows += [jnp.exp(opened + since) * scale[2 + near + m] for m in range(far)]
        totals.append(last + (shut[b][0] + shut[b][1]))
        terms = halves(stack_rows(rows))
        coefs[tokens_here, :] = terms

        span_queries = queries[tokens_here, :]
        scores = jnp.where(causal, dot(span_queries, keys[tokens_here, :], ((1,), (1,))), 0.0)
        gaps = dot(terms[:, :LANES], place)
        block = values[tokens_here, column : column + width]
        parts = []
        for part in range(width // LANES):
            here = block[:, part * LANES : (part + 1) * LANES]
            left, right = [], []
            for inner in range(per_tile):
                head = part * per_tile + inner
                gap = gaps[:, head * TILE : (head + 1) * TILE] - sums[head : head + 1, :]
                left.append((jnp.exp(jnp.minimum(gap, 80.0)) * scores).astype(jnp.bfloat16))
                right.append(jnp.where(lane_head == inner, here, jnp.zeros_like(here)))
            parts.append(dot(jnp.concatenate(left, axis=1), jnp.concatenate(right, axis=0)))
        mixed = jnp.concatenate(parts, axis=1)
        for k in levels:
            mixed += dot(terms, hot[k]) * dot(span_queries, slots[k].astype(jnp.bfloat16))
        out[tokens_here, :] = mixed

        if b == tiles - 1:
            break
        scaled = (block.astype(jnp.float32) * dot(terms, hot[near])).astype(jnp.bfloat16)
        now = dot(keys[tokens_here, :], scaled, ((0,), (0,)))
        for k in range(near):
            if not (b >> k) & 1:
                slots[k] = now
                break
            since = sum(totals[(b >> k) << k :])
            now = now + slots[k] * head_row(jnp.exp(since)[:, :1], width, head_dim)


def gate_kernel(head_dim, heads, first, column, xor, me, local, coefs, queries, states, gate, *outs):
    count = len(outs) if xor else outs[0].shape[0]
    rows = local.shape[0] // count
    far, _, width = states.shape
    hot = [spread(first + m * heads, width, head_dim) for m in range(far)]
    arrived = [states[m] for m in range(far)]

    def rows_of(place):
        start = place * rows
        here = pl.ds(pl.multiple_of(start, rows), rows)
        total = local[here, :]
        for m in range(far):
            total += dot(coefs[here, :], hot[m]) * dot(queries[here, :], arrived[m])
        opened = 0.5 * gate[here, column : column + width].astype(jnp.float32)
        return (total * opened * (1.0 + jnp.tanh(opened))).astype(jnp.bfloat16)

    if xor:
        for index, out in enumerate(outs):
            out[...] = rows_of(jnp.bitwise_xor(me[0], index))
    else:

        @pl.loop(0, count)
        def _(index):
            outs[0][index] = rows_of(index)


def norm_kernel(sources, me, gain, *rest):
    out = rest[-1]
    step = pl.program_id(0)

    def write(blocks):
        blocks = [block.astype(jnp.float32) for block in blocks]
        count = sum(block.shape[1] for block in blocks)
        square = sum(jnp.sum(block * block, axis=1, keepdims=True) for block in blocks)
        scale = lax.rsqrt(square / count + 1e-05)
        at = 0
        for block in blocks:
            end = at + block.shape[1]
            out[:, at:end] = (block * scale * gain[:, at:end]).astype(out.dtype)
            at = end

    if sources is None:
        parts = rest[:-1]
        write([part[index] for index in range(parts[0].shape[0]) for part in parts])
        return
    for index, places in enumerate(sources):

        @pl.when(step == index)
        def _(places=places):
            write([rest[place][...] for place in places])


def params(limit):
    return pltpu.CompilerParams(vmem_limit_bytes=limit * MIB)


def body(values, gate_z, b_keys, c_queries, log_decay, level_weight, doc_start, norm_gain):
    tokens, width = values.shape
    heads_here = log_decay.shape[1]
    head_dim = width // heads_here
    state_size = b_keys.shape[2]
    tiles = tokens // TILE
    near = tiles.bit_length() - 1
    seq_count = lax.axis_size("seq")
    far = seq_count.bit_length() - 1
    head_count = lax.axis_size("head")
    head_index = lax.axis_index("head")
    group_index = head_index * heads_here // (MIXER_HEADS // GROUPS)
    key_rows = lax.dynamic_index_in_dim(b_keys, group_index, 1, keepdims=False)
    query_rows = lax.dynamic_index_in_dim(c_queries, group_index, 1, keepdims=False)
    decay = jnp.transpose(log_decay)
    weight = jnp.transpose(level_weight, (2, 1, 0))
    heads = SUBLANES
    if heads_here < heads:
        short = heads - heads_here
        decay = jnp.pad(decay, ((0, short), (0, 0)))
        weight = jnp.pad(weight, ((0, 0), (0, short), (0, 0)), constant_values=1.0)
    chunks = max(1, heads_here // heads)
    part = width // chunks
    levels = weight.shape[0]
    smem = pl.BlockSpec(memory_space=pltpu.SMEM)
    decays = [decay[c * heads : (c + 1) * heads] for c in range(chunks)]
    weights = [weight[:, c * heads : (c + 1) * heads] for c in range(chunks)]

    whole = pl.BlockSpec(memory_space=pltpu.VMEM)
    anywhere = pl.BlockSpec(memory_space=pl.ANY)

    def state_call(c):
        pieces = min(4, tiles)
        return pl.pallas_call(
            functools.partial(state_kernel, head_dim, c * part, pieces),
            in_specs=[smem, whole, whole, anywhere],
            out_specs=[whole, whole, whole],
            out_shape=[
                jax.ShapeDtypeStruct((state_size, part), jnp.float32),
                jax.ShapeDtypeStruct((state_size, part), jnp.bfloat16),
                jax.ShapeDtypeStruct((SUBLANES, part), jnp.float32),
            ],
            scratch_shapes=[
                pltpu.VMEM((tokens, part), jnp.bfloat16),
                pltpu.SemaphoreType.DMA((pieces,)),
            ],
            compiler_params=params(16),
            cost_estimate=pl.CostEstimate(
                flops=4 * tokens * state_size * part, bytes_accessed=3 * tokens * part, transcendentals=0
            ),
            name="block_state",
        )(doc_start, decays[c], key_rows, values)

    def local_call(c, follow):
        return pl.pallas_call(
            functools.partial(local_kernel, head_dim, c * part, far),
            in_specs=[smem, whole, whole, whole, whole, whole, anywhere],
            out_specs=[whole, whole],
            out_shape=[
                jax.ShapeDtypeStruct((tokens, part), jnp.float32),
                jax.ShapeDtypeStruct((tokens, 2 * LANES), jnp.bfloat16),
            ],
            compiler_params=params(16),
            cost_estimate=pl.CostEstimate(
                flops=16 * tokens * state_size * part, bytes_accessed=12 * tokens * part, transcendentals=0
            ),
            name="local_mixer",
        )(doc_start, decays[c], weights[c], values, query_rows, key_rows, follow)

    rows = tokens // head_count
    direct = head_count == GROUPS
    me = jnp.reshape(head_index, (1,)).astype(jnp.int32)

    def gate_call(c, local, coefs, states):
        if direct:
            out_shape = [jax.ShapeDtypeStruct((rows, part), jnp.bfloat16)] * head_count
        else:
            out_shape = [jax.ShapeDtypeStruct((head_count, rows, part), jnp.bfloat16)]
        return pl.pallas_call(
            functools.partial(gate_kernel, head_dim, heads, (near + 7) * heads, c * part, direct),
            in_specs=[smem, whole, whole, whole, whole, whole],
            out_specs=[whole] * len(out_shape),
            out_shape=out_shape,
            compiler_params=params(16),
            cost_estimate=pl.CostEstimate(
                flops=4 * tokens * state_size * part, bytes_accessed=8 * tokens * part, transcendentals=0
            ),
            name="far_and_gate",
        )(me, local, coefs, query_rows, states, gate_z)

    owns, throughs, messages = zip(*[(s, t[:1], m) for s, m, t in map(state_call, range(chunks))])
    owns = list(owns)
    carried = [[None] * far for _ in range(chunks)]
    locals_ = [local_call(0, messages[-1])]
    for bit in range(far):
        size = 2**bit
        for c in range(chunks):
            moving = messages[c] if bit == 0 else owns[c].astype(jnp.bfloat16)
            if bit == 1 and len(locals_) == c and c:
                locals_.append(local_call(c, moving))
            arrived = None
            for hop in range(1, size + 1):
                source = [base + size + hop - 2 for base in range(0, seq_count, 2 * size)]
                got = lax.ppermute(moving, "seq", [(s, s + 1) for s in source])
                arrived = got if arrived is None else arrived + got
                passed = got.astype(jnp.float32) * throughs[c]
                moving = passed.astype(jnp.bfloat16)
            carried[c][bit] = arrived
            owns[c] = owns[c] + passed
    for c in range(len(locals_), chunks):
        locals_.append(local_call(c, messages[-1]))

    pieces = []
    for c in range(chunks):
        local, coefs = locals_[c]
        out = gate_call(c, local, coefs, jnp.stack(carried[c]))
        if direct:
            got = [out[0]] + [None] * (head_count - 1)
            for apart in sorted(range(1, head_count), key=lambda k: -k.bit_count() * 8 - k):
                pairs = [(source, source ^ apart) for source in range(head_count)]
                got[apart] = lax.ppermute(out[apart], "head", pairs)
            pieces.append(got)
        else:
            pieces.append(lax.all_to_all(out[0], "head", split_axis=0, concat_axis=0))

    gain = jnp.reshape(norm_gain, (1, -1))
    group_width = width * head_count // GROUPS
    if direct:
        flat = [piece for got in pieces for piece in got]
        sources = [[c * head_count + k for c in range(chunks)] for k in range(head_count)]
        column = lambda i, s: (0, jnp.bitwise_xor(i, s[0]))
        in_specs = [pl.BlockSpec((rows, part), lambda i, s: (0, 0))] * len(flat)
    else:
        flat = pieces
        sources = None
        per_group = max(1, group_width // width)
        column = lambda i, s: (0, i)
        in_specs = [pl.BlockSpec((per_group, rows, part), lambda i, s: (i, 0, 0))] * len(flat)
    return pl.pallas_call(
        functools.partial(norm_kernel, sources),
        grid_spec=pltpu.PrefetchScalarGridSpec(
            num_scalar_prefetch=1,
            grid=(GROUPS,),
            in_specs=[pl.BlockSpec((1, group_width), column)] + in_specs,
            out_specs=pl.BlockSpec((rows, group_width), column),
        ),
        out_shape=jax.ShapeDtypeStruct((rows, width * head_count), jnp.bfloat16),
        compiler_params=params(16),
        cost_estimate=pl.CostEstimate(
            flops=8 * tokens * width, bytes_accessed=4 * tokens * width, transcendentals=0
        ),
        name="norm_rows",
    )(me, gain, *flat)


def solution(mesh):
    in_specs = (
        P("seq", "head"),
        P("seq", "head"),
        P("seq", None, None),
        P("seq", None, None),
        P("seq", "head"),
        P("seq", "head", None),
        P(),
        P(),
    )
    out_specs = P(("seq", "head"), None)
    return jax.shard_map(body, mesh=mesh, in_specs=in_specs, out_specs=out_specs, check_vma=False)
```

```python
import functools

import jax
import jax.numpy as jnp
from jax import lax
from jax.experimental import pallas as pl
from jax.experimental.pallas import tpu as pltpu
from jax.sharding import PartitionSpec as P

MIXER_HEADS = 128
GROUPS = 8
SPAN = 64
TILE = 2 * SPAN
LANES = 128
SUBLANES = 8
NEVER = -1e30
HIGHEST = lax.Precision.HIGHEST
MIB = 2**20


def dot(left, right, contract=((1,), (0,)), precision=None):
    return lax.dot_general(
        left, right, (contract, ((), ())), precision=precision, preferred_element_type=jnp.float32
    )


def iota(shape, axis):
    return lax.broadcasted_iota(jnp.int32, shape, axis)


def halves(coef):
    high = coef.astype(jnp.bfloat16)
    low = (coef - high.astype(jnp.float32)).astype(jnp.bfloat16)
    return jnp.concatenate([high, low], axis=1)


def spread(first, width, head_dim):
    row = jnp.bitwise_and(iota((2 * LANES, width), 0), LANES - 1)
    head = jnp.right_shift(iota((2 * LANES, width), 1), head_dim.bit_length() - 1)
    return jnp.where(row == head + first, 1.0, 0.0).astype(jnp.bfloat16)


def head_row(column, width, head_dim):
    shape = (column.shape[0], width)
    head = jnp.right_shift(iota(shape, 1), head_dim.bit_length() - 1)
    return jnp.sum(jnp.where(head == iota(shape, 0), column, 0.0), axis=0, keepdims=True)


def stack_rows(pieces):
    rows = sum(piece.shape[0] for piece in pieces)
    if rows < LANES:
        pieces = pieces + [jnp.zeros((LANES - rows, LANES), jnp.float32)]
    return jnp.transpose(jnp.concatenate(pieces, axis=0))


def tile_rows(decay):
    tiles = decay.shape[1] // TILE
    return jnp.concatenate([decay[:, b * TILE : (b + 1) * TILE] for b in range(tiles)], axis=0)


def resets(docs, tiles):
    first = lax.axis_index("seq") * (tiles * (TILE // SPAN))
    shut = [NEVER * docs[first + s].astype(jnp.float32) for s in range(tiles * (TILE // SPAN))]
    return [shut[2 * b : 2 * b + 2] for b in range(tiles)]


def state_kernel(
    head_dim,
    chunk,
    pieces,
    docs_far,
    decay_far,
    keys,
    values,
    state,
    message,
    through,
    docs,
    decay,
    inputs,
    arrived,
):
    heads, tokens = decay.shape
    width = inputs.shape[1]
    column = chunk * width
    small = [
        pltpu.make_async_copy(
            decay_far.at[pl.ds(chunk * heads, heads), :], decay, arrived.at[pieces]
        ),
        pltpu.make_async_copy(docs_far, docs, arrived.at[pieces + 1]),
    ]
    tiles = tokens // TILE
    rows = tokens // pieces
    copies = [
        pltpu.make_async_copy(
            values.at[pl.ds(i * rows, rows), pl.ds(column, width)],
            inputs.at[pl.ds(i * rows, rows), :],
            arrived.at[i],
        )
        for i in range(pieces)
    ]
    for copy in small + copies:
        copy.start()
    for copy in small:
        copy.wait()
    shut = resets(docs, tiles)
    lane = iota((heads, TILE), 1)
    later = jnp.where(iota((TILE, TILE), 0) > iota((TILE, TILE), 1), 1.0, 0.0)
    stacked = tile_rows(decay)
    suffix = dot(stacked, later, precision=HIGHEST)
    totals = jnp.sum(stacked, axis=1, keepdims=True)
    after = jnp.zeros((heads, 1), jnp.float32)
    closed = jnp.float32(0.0)
    scales = [None] * tiles
    for b in reversed(range(tiles)):
        ends = jnp.where(lane < SPAN, closed + shut[b][1], closed)
        scales[b] = jnp.exp(suffix[b * heads : (b + 1) * heads] + after + ends)
        closed = closed + shut[b][1] + shut[b][0]
        after = after + totals[b * heads : (b + 1) * heads]
    terms = halves(stack_rows(scales))
    row = head_row(jnp.exp(after + closed), width, head_dim)
    through[...] = jnp.broadcast_to(row, through.shape)
    owner = jnp.right_shift(
        jnp.bitwise_and(iota((1, 2 * LANES), 1), LANES - 1), heads.bit_length() - 1
    )
    shape = (2 * LANES, width)
    same = jnp.bitwise_and(iota(shape, 0), heads - 1) == jnp.right_shift(
        iota(shape, 1), head_dim.bit_length() - 1
    )
    one_hot = jnp.where(same, 1.0, 0.0).astype(jnp.bfloat16)
    chosen = [
        terms * jnp.where(owner == b, 1.0, 0.0).astype(jnp.bfloat16) for b in range(tiles)
    ]
    total = jnp.zeros(state.shape, jnp.float32)
    for i in range(pieces):
        span = tiles // pieces
        scale = dot(jnp.concatenate(chosen[i * span : (i + 1) * span], axis=0), one_hot)
        copies[i].wait()
        scaled = inputs[i * rows : (i + 1) * rows, :].astype(jnp.float32) * scale
        total += dot(
            keys[i * rows : (i + 1) * rows, :], scaled.astype(jnp.bfloat16), ((0,), (0,))
        )
    state[...] = total
    message[...] = total.astype(jnp.bfloat16)


def local_kernel(
    head_dim, heads, chunk, far, docs, decay, weight, values, queries, keys, follow, out, coefs
):
    del follow
    tokens, width = out.shape
    column = chunk * width
    mine = slice(chunk * heads, (chunk + 1) * heads)
    tiles = tokens // TILE
    near = tiles.bit_length() - 1
    shut = resets(docs, tiles)
    lane = iota((heads, TILE), 1)
    upto = jnp.where(iota((TILE, TILE), 0) <= iota((TILE, TILE), 1), 1.0, 0.0)
    all_sums = dot(tile_rows(decay[mine, :]), upto, precision=HIGHEST)
    causal = iota((TILE, TILE), 0) >= iota((TILE, TILE), 1)
    per_tile = LANES // head_dim
    lane_head = jnp.right_shift(iota((TILE, LANES), 1), head_dim.bit_length() - 1)
    shape = (LANES, heads * TILE)
    row, col = iota(shape, 0), iota(shape, 1)
    group = jnp.right_shift(row, heads.bit_length() - 1)
    fits = jnp.bitwise_and(row, heads - 1) == jnp.right_shift(col, TILE.bit_length() - 1)
    older = jnp.bitwise_and(col, TILE - 1) < SPAN
    low, high = jnp.where(older, 3, 0), jnp.where(older, 6, 3)
    place = fits & (group >= low) & (group < high)
    place = jnp.where(place, 1.0, 0.0).astype(jnp.bfloat16)
    hot = [spread((6 + i) * heads, width, head_dim) for i in range(near + 1)]

    totals, slots = [], [None] * near
    for b in range(tiles):
        tokens_here = slice(b * TILE, (b + 1) * TILE)
        sums = all_sums[b * heads : (b + 1) * heads]
        scale = [weight[level, mine, tokens_here] for level in range(weight.shape[0])]
        last = jnp.broadcast_to(sums[:, TILE - 1 :], sums.shape)
        opened = sums + jnp.where(lane < SPAN, shut[b][0], shut[b][0] + shut[b][1])
        own = sums + jnp.log(scale[0])
        beside = jnp.where(lane < SPAN, own, sums + jnp.log(scale[1]) + shut[b][1])
        rows = []
        for value in (own, beside):
            for _ in range(3):
                term = value.astype(jnp.bfloat16).astype(jnp.float32)
                rows.append(term)
                value = value - term
        levels = [k for k in range(near) if (b >> k) & 1]
        for k in range(near):
            if k in levels:
                since = sum(totals[(b >> k) << k : b], jnp.zeros_like(sums))
                rows.append(jnp.exp(opened + since) * scale[2 + k])
            else:
                rows.append(jnp.zeros_like(sums))
        rows.append(jnp.exp(last - sums + jnp.where(lane < SPAN, shut[b][1], 0.0)))
        since = sum(totals, jnp.zeros_like(sums))
        rows += [jnp.exp(opened + since) * scale[2 + near + m] for m in range(far)]
        totals.append(last + (shut[b][0] + shut[b][1]))
        terms = halves(stack_rows(rows))
        coefs[tokens_here, :] = terms

        span_queries = queries[tokens_here, :]
        scores = jnp.where(causal, dot(span_queries, keys[tokens_here, :], ((1,), (1,))), 0.0)
        gaps = dot(terms[:, :LANES], place)
        block = values[tokens_here, column : column + width]
        parts = []
        for part in range(width // LANES):
            here = block[:, part * LANES : (part + 1) * LANES]
            left, right = [], []
            for inner in range(per_tile):
                head = part * per_tile + inner
                gap = gaps[:, head * TILE : (head + 1) * TILE] - sums[head : head + 1, :]
                left.append((jnp.exp(jnp.minimum(gap, 80.0)) * scores).astype(jnp.bfloat16))
                right.append(jnp.where(lane_head == inner, here, jnp.zeros_like(here)))
            parts.append(dot(jnp.concatenate(left, axis=1), jnp.concatenate(right, axis=0)))
        mixed = jnp.concatenate(parts, axis=1)
        for k in levels:
            mixed += dot(terms, hot[k]) * dot(span_queries, slots[k].astype(jnp.bfloat16))
        out[tokens_here, :] = mixed

        if b == tiles - 1:
            break
        scaled = (block.astype(jnp.float32) * dot(terms, hot[near])).astype(jnp.bfloat16)
        now = dot(keys[tokens_here, :], scaled, ((0,), (0,)))
        for k in range(near):
            if not (b >> k) & 1:
                slots[k] = now
                break
            since = sum(totals[(b >> k) << k :])
            now = now + slots[k] * head_row(jnp.exp(since)[:, :1], width, head_dim)


def gate_kernel(head_dim, heads, first, column, xor, me, local, coefs, queries, states, gate, *outs):
    count = len(outs) if xor else outs[0].shape[0]
    rows = local.shape[0] // count
    far, _, width = states.shape
    hot = [spread(first + m * heads, width, head_dim) for m in range(far)]
    arrived = [states[m] for m in range(far)]

    def rows_of(place):
        start = place * rows
        here = pl.ds(pl.multiple_of(start, rows), rows)
        total = local[here, :]
        for m in range(far):
            total += dot(coefs[here, :], hot[m]) * dot(queries[here, :], arrived[m])
        opened = 0.5 * gate[here, column : column + width].astype(jnp.float32)
        return (total * opened * (1.0 + jnp.tanh(opened))).astype(jnp.bfloat16)

    if xor:
        for index, out in enumerate(outs):
            out[...] = rows_of(jnp.bitwise_xor(me[0], index))
    else:

        @pl.loop(0, count)
        def _(index):
            outs[0][index] = rows_of(index)


def norm_kernel(sources, before, me, gain, *rest):
    out = rest[-1]
    step = pl.program_id(0)

    def write(blocks):
        blocks = [block.astype(jnp.float32) for block in blocks]
        count = sum(block.shape[1] for block in blocks)
        square = sum(jnp.sum(block * block, axis=1, keepdims=True) for block in blocks)
        scale = lax.rsqrt(square / count + 1e-05)
        at = 0
        for block in blocks:
            end = at + block.shape[1]
            out[:, at:end] = (block * scale * gain[:, at:end]).astype(out.dtype)
            at = end

    if sources is None:
        parts = rest[:-1]
        write([part[index] for index in range(parts[0].shape[0]) for part in parts])
        return
    for index, places in enumerate(sources):

        @pl.when(step == index)
        def _(places=places):
            write([rest[before + place][...] for place in places])


def partners(count):
    return sorted(range(1, count), key=lambda apart: (-apart.bit_count(), -apart))


def params(limit):
    return pltpu.CompilerParams(vmem_limit_bytes=limit * MIB)


def body(values, gate_z, b_keys, c_queries, log_decay, level_weight, doc_start, norm_gain):
    tokens, width = values.shape
    heads_here = log_decay.shape[1]
    head_dim = width // heads_here
    state_size = b_keys.shape[2]
    tiles = tokens // TILE
    near = tiles.bit_length() - 1
    seq_count = lax.axis_size("seq")
    far = seq_count.bit_length() - 1
    head_count = lax.axis_size("head")
    head_index = lax.axis_index("head")
    group_index = head_index * heads_here // (MIXER_HEADS // GROUPS)
    key_rows = lax.dynamic_index_in_dim(b_keys, group_index, 1, keepdims=False)
    query_rows = lax.dynamic_index_in_dim(c_queries, group_index, 1, keepdims=False)
    decay = jnp.transpose(log_decay)
    weight = jnp.transpose(level_weight, (2, 1, 0))
    heads = SUBLANES
    if heads_here < heads:
        short = heads - heads_here
        decay = jnp.pad(decay, ((0, short), (0, 0)))
        weight = jnp.pad(weight, ((0, 0), (0, short), (0, 0)), constant_values=1.0)
    chunks = max(1, heads_here // heads)
    part = width // chunks
    levels = weight.shape[0]
    smem = pl.BlockSpec(memory_space=pltpu.SMEM)

    whole = pl.BlockSpec(memory_space=pltpu.VMEM)
    anywhere = pl.BlockSpec(memory_space=pl.ANY)
    far_away = pl.BlockSpec(memory_space=pltpu.HBM)

    def state_call(c):
        pieces = min(4, tiles)
        return pl.pallas_call(
            functools.partial(state_kernel, head_dim, c, pieces),
            in_specs=[far_away, far_away, whole, far_away],
            out_specs=[whole, whole, whole],
            out_shape=[
                jax.ShapeDtypeStruct((state_size, part), jnp.float32),
                jax.ShapeDtypeStruct((state_size, part), jnp.bfloat16),
                jax.ShapeDtypeStruct((SUBLANES, part), jnp.float32),
            ],
            scratch_shapes=[
                pltpu.SMEM(doc_start.shape, doc_start.dtype),
                pltpu.VMEM((heads, tokens), jnp.float32),
                pltpu.VMEM((tokens, part), jnp.bfloat16),
                pltpu.SemaphoreType.DMA((pieces + 2,)),
            ],
            compiler_params=params(16),
            cost_estimate=pl.CostEstimate(
                flops=4 * tokens * state_size * part, bytes_accessed=3 * tokens * part, transcendentals=0
            ),
            name="block_state",
        )(doc_start, decay, key_rows, values)

    def local_call(c, follow):
        return pl.pallas_call(
            functools.partial(local_kernel, head_dim, heads, c, far),
            in_specs=[smem, whole, whole, whole, whole, whole, anywhere],
            out_specs=[whole, whole],
            out_shape=[
                jax.ShapeDtypeStruct((tokens, part), jnp.float32),
                jax.ShapeDtypeStruct((tokens, 2 * LANES), jnp.bfloat16),
            ],
            compiler_params=params(16),
            cost_estimate=pl.CostEstimate(
                flops=16 * tokens * state_size * part, bytes_accessed=12 * tokens * part, transcendentals=0
            ),
            name="local_mixer",
        )(doc_start, decay, weight, values, query_rows, key_rows, follow)

    rows = tokens // head_count
    direct = head_count == GROUPS
    me = jnp.reshape(head_index, (1,)).astype(jnp.int32)

    def gate_call(c, local, coefs, states):
        if direct:
            out_shape = [jax.ShapeDtypeStruct((rows, part), jnp.bfloat16)] * head_count
        else:
            out_shape = [jax.ShapeDtypeStruct((head_count, rows, part), jnp.bfloat16)]
        return pl.pallas_call(
            functools.partial(gate_kernel, head_dim, heads, (near + 7) * heads, c * part, direct),
            in_specs=[smem, whole, whole, whole, whole, whole],
            out_specs=[whole] * len(out_shape),
            out_shape=out_shape,
            compiler_params=params(16),
            cost_estimate=pl.CostEstimate(
                flops=4 * tokens * state_size * part, bytes_accessed=8 * tokens * part, transcendentals=0
            ),
            name="far_and_gate",
        )(me, local, coefs, query_rows, states, gate_z)

    owns, throughs, messages = zip(*[(s, t[:1], m) for s, m, t in map(state_call, range(chunks))])
    owns = list(owns)
    carried = [[None] * far for _ in range(chunks)]
    second = messages[0]
    for bit in range(far):
        size = 2**bit
        for c in range(chunks):
            moving = messages[c] if bit == 0 else owns[c].astype(jnp.bfloat16)
            if bit == 1 and c == 0:
                second = moving
            arrived = None
            for hop in range(1, size + 1):
                source = [base + size + hop - 2 for base in range(0, seq_count, 2 * size)]
                got = lax.ppermute(moving, "seq", [(s, s + 1) for s in source])
                arrived = got if arrived is None else arrived + got
                passed = got.astype(jnp.float32) * throughs[c]
                moving = passed.astype(jnp.bfloat16)
            carried[c][bit] = arrived
            owns[c] = owns[c] + passed

    pieces = []
    follow = second
    for c in range(chunks):
        local, coefs = local_call(c, follow)
        out = gate_call(c, local, coefs, jnp.stack(carried[c]))
        follow = out[0]
        if direct:
            got = [out[0]] + [None] * (head_count - 1)
            for apart in partners(head_count):
                pairs = [(source, source ^ apart) for source in range(head_count)]
                got[apart] = lax.ppermute(out[apart], "head", pairs)
            pieces.append(got)
        else:
            pieces.append(lax.all_to_all(out[0], "head", split_axis=0, concat_axis=0))

    gain = jnp.reshape(norm_gain, (1, -1))
    group_width = width * head_count // GROUPS

    def norm_call(kernel, steps, column, in_specs, operands, result=None):
        given = [] if result is None else [result]
        return pl.pallas_call(
            kernel,
            grid_spec=pltpu.PrefetchScalarGridSpec(
                num_scalar_prefetch=1,
                grid=(steps,),
                in_specs=[pl.BlockSpec((1, group_width), column)] + [far_away] * len(given) + in_specs,
                out_specs=pl.BlockSpec((rows, group_width), column),
            ),
            out_shape=jax.ShapeDtypeStruct((rows, width * head_count), jnp.bfloat16),
            input_output_aliases={2: 0} if given else {},
            compiler_params=params(16),
            cost_estimate=pl.CostEstimate(
                flops=8 * rows * group_width * steps,
                bytes_accessed=4 * rows * group_width * steps,
                transcendentals=0,
            ),
            name="norm_rows",
        )(me, gain, *given, *operands)

    if not direct:
        per_group = max(1, group_width // width)
        spec = pl.BlockSpec((per_group, rows, part), lambda i, s: (i, 0, 0))
        kernel = functools.partial(norm_kernel, None, 0)
        return norm_call(kernel, GROUPS, lambda i, s: (0, i), [spec] * chunks, pieces)
    order = [0] + partners(head_count)
    early = order[: 3 * head_count // 4]
    result = None
    for some in (early, order[len(early) :]):
        operands = [pieces[c][k] for k in some for c in range(chunks)]
        sources = [[n * chunks + c for c in range(chunks)] for n in range(len(some))]

        def column(i, s, some=some):
            apart = sum(jnp.where(i == n, k, 0) for n, k in enumerate(some))
            return 0, jnp.bitwise_xor(apart, s[0])

        kernel = functools.partial(norm_kernel, sources, 0 if result is None else 1)
        result = norm_call(kernel, len(some), column, [whole] * len(operands), operands, result)
    return result


def solution(mesh):
    in_specs = (
        P("seq", "head"),
        P("seq", "head"),
        P("seq", None, None),
        P("seq", None, None),
        P("seq", "head"),
        P("seq", "head", None),
        P(),
        P(),
    )
    out_specs = P(("seq", "head"), None)
    return jax.shard_map(body, mesh=mesh, in_specs=in_specs, out_specs=out_specs, check_vma=False)
```

```python
import functools

import jax
import jax.numpy as jnp
from jax import lax
from jax.experimental import pallas as pl
from jax.experimental.pallas import tpu as pltpu
from jax.sharding import PartitionSpec as P

MIXER_HEADS = 128
GROUPS = 8
SPAN = 64
TILE = 2 * SPAN
LANES = 128
WIDE = 2 * LANES
SUBLANES = 8
NEVER = -1e30
HIGHEST = lax.Precision.HIGHEST
MIB = 2**20


def dot(left, right, contract=((1,), (0,)), precision=None):
    return lax.dot_general(
        left, right, (contract, ((), ())), precision=precision, preferred_element_type=jnp.float32
    )


def iota(shape, axis):
    return lax.broadcasted_iota(jnp.int32, shape, axis)


def halves(coef):
    high = coef.astype(jnp.bfloat16)
    low = (coef - high.astype(jnp.float32)).astype(jnp.bfloat16)
    return jnp.concatenate([high, low], axis=1)


def spread(first, width, head_dim):
    row = jnp.bitwise_and(iota((2 * LANES, width), 0), LANES - 1)
    head = jnp.right_shift(iota((2 * LANES, width), 1), head_dim.bit_length() - 1)
    return jnp.where(row == head + first, 1.0, 0.0).astype(jnp.bfloat16)


def head_row(column, width, head_dim):
    shape = (column.shape[0], width)
    head = jnp.right_shift(iota(shape, 1), head_dim.bit_length() - 1)
    return jnp.sum(jnp.where(head == iota(shape, 0), column, 0.0), axis=0, keepdims=True)


def stack_rows(pieces):
    rows = sum(piece.shape[0] for piece in pieces)
    if rows < LANES:
        pieces = pieces + [jnp.zeros((LANES - rows, LANES), jnp.float32)]
    return jnp.transpose(jnp.concatenate(pieces, axis=0))


def tile_rows(decay):
    tiles = decay.shape[1] // TILE
    return jnp.concatenate([decay[:, b * TILE : (b + 1) * TILE] for b in range(tiles)], axis=0)


def resets(docs, tiles):
    first = lax.axis_index("seq") * (tiles * (TILE // SPAN))
    shut = [NEVER * docs[first + s].astype(jnp.float32) for s in range(tiles * (TILE // SPAN))]
    return [shut[2 * b : 2 * b + 2] for b in range(tiles)]


def pack(total, through):
    high = through.astype(jnp.bfloat16)
    low = (through - high.astype(jnp.float32)).astype(jnp.bfloat16)
    return jnp.concatenate([total.astype(jnp.bfloat16), high, low], axis=0)


def state_kernel(
    head_dim,
    chunk,
    pieces,
    docs_far,
    decay_far,
    keys,
    values,
    follow,
    state,
    message,
    through,
    docs,
    decay,
    inputs,
    arrived,
):
    del follow
    heads, tokens = decay.shape
    width = inputs.shape[1]
    column = chunk * width
    small = [
        pltpu.make_async_copy(
            decay_far.at[pl.ds(chunk * heads, heads), :], decay, arrived.at[pieces]
        ),
        pltpu.make_async_copy(docs_far, docs, arrived.at[pieces + 1]),
    ]
    tiles = tokens // TILE
    rows = tokens // pieces
    copies = [
        pltpu.make_async_copy(
            values.at[pl.ds(i * rows, rows), pl.ds(column, width)],
            inputs.at[pl.ds(i * rows, rows), :],
            arrived.at[i],
        )
        for i in range(pieces)
    ]
    for copy in small + copies:
        copy.start()
    for copy in small:
        copy.wait()
    shut = resets(docs, tiles)
    lane = iota((heads, TILE), 1)
    later = jnp.where(iota((TILE, TILE), 0) > iota((TILE, TILE), 1), 1.0, 0.0)
    stacked = tile_rows(decay)
    suffix = dot(stacked, later, precision=HIGHEST)
    totals = jnp.sum(stacked, axis=1, keepdims=True)
    after = jnp.zeros((heads, 1), jnp.float32)
    closed = jnp.float32(0.0)
    scales = [None] * tiles
    for b in reversed(range(tiles)):
        ends = jnp.where(lane < SPAN, closed + shut[b][1], closed)
        scales[b] = jnp.exp(suffix[b * heads : (b + 1) * heads] + after + ends)
        closed = closed + shut[b][1] + shut[b][0]
        after = after + totals[b * heads : (b + 1) * heads]
    terms = halves(stack_rows(scales))
    row = head_row(jnp.exp(after + closed), width, head_dim)
    through[...] = jnp.broadcast_to(row, through.shape)
    owner = jnp.right_shift(
        jnp.bitwise_and(iota((1, 2 * LANES), 1), LANES - 1), heads.bit_length() - 1
    )
    shape = (2 * LANES, width)
    same = jnp.bitwise_and(iota(shape, 0), heads - 1) == jnp.right_shift(
        iota(shape, 1), head_dim.bit_length() - 1
    )
    one_hot = jnp.where(same, 1.0, 0.0).astype(jnp.bfloat16)
    chosen = [
        terms * jnp.where(owner == b, 1.0, 0.0).astype(jnp.bfloat16) for b in range(tiles)
    ]
    total = jnp.zeros(state.shape, jnp.float32)
    for i in range(pieces):
        span = tiles // pieces
        scale = dot(jnp.concatenate(chosen[i * span : (i + 1) * span], axis=0), one_hot)
        copies[i].wait()
        scaled = inputs[i * rows : (i + 1) * rows, :].astype(jnp.float32) * scale
        total += dot(
            keys[i * rows : (i + 1) * rows, :], scaled.astype(jnp.bfloat16), ((0,), (0,))
        )
    state[...] = total
    message[...] = pack(total, through[...])


def merge_kernel(bit, arrivals, follow, *refs):
    del follow
    got, (own, through, before, new_own, new_through, new_before, message) = (
        refs[:arrivals],
        refs[arrivals:],
    )
    states = own.shape[0]
    total = sum(part[...].astype(jnp.float32) for part in got)
    decays = total[states : states + SUBLANES] + total[states + SUBLANES :]
    upper = jnp.bitwise_and(jnp.right_shift(lax.axis_index("seq"), bit), 1).astype(jnp.float32)
    new_before[...] = before[...] * (decays + (1.0 - upper))
    summed = own[...] + total[:states] * through[:1]
    passed = through[...] * (decays + (1.0 - upper))
    new_own[...] = summed
    new_through[...] = passed
    message[...] = pack(summed, passed)


def local_kernel(
    head_dim, heads, chunk, far, docs, decay, weight, values, queries, keys, *rest
):
    out, coefs = rest[-2:]
    tokens, width = out.shape
    column = chunk * width
    mine = slice(chunk * heads, (chunk + 1) * heads)
    tiles = tokens // TILE
    near = tiles.bit_length() - 1
    shut = resets(docs, tiles)
    lane = iota((heads, TILE), 1)
    upto = jnp.where(iota((TILE, TILE), 0) <= iota((TILE, TILE), 1), 1.0, 0.0)
    all_sums = dot(tile_rows(decay[mine, :]), upto, precision=HIGHEST)
    causal = iota((TILE, TILE), 0) >= iota((TILE, TILE), 1)
    early = iota((SPAN, TILE), 1) < SPAN
    per_tile = LANES // head_dim
    lane_head = jnp.right_shift(iota((TILE, LANES), 1), head_dim.bit_length() - 1)
    hot = [spread((2 + i) * heads, width, head_dim) for i in range(near + 1)]

    def here(b):
        return slice(b * TILE, (b + 1) * TILE)

    columns, totals = [], []
    for b in range(tiles):
        sums = all_sums[b * heads : (b + 1) * heads]
        scale = [weight[level, mine, here(b)] for level in range(weight.shape[0])]
        last = jnp.broadcast_to(sums[:, TILE - 1 :], sums.shape)
        opened = sums + jnp.where(lane < SPAN, shut[b][0], shut[b][0] + shut[b][1])
        rows = [sums + jnp.log(scale[0]), sums + jnp.log(scale[1]) + shut[b][1]]
        for k in range(near):
            if (b >> k) & 1:
                since = sum(totals[(b >> k) << k : b], jnp.zeros_like(sums))
                rows.append(jnp.exp(opened + since) * scale[2 + k])
            else:
                rows.append(jnp.zeros_like(sums))
        rows.append(jnp.exp(last - sums + jnp.where(lane < SPAN, shut[b][1], 0.0)))
        since = sum(totals, jnp.zeros_like(sums))
        rows += [jnp.exp(opened + since) * scale[2 + near + m] for m in range(far)]
        totals.append(last + (shut[b][0] + shut[b][1]))
        columns.append(stack_rows(rows))
        coefs[here(b), :] = halves(columns[b])

    whole = (tiles - 1) * TILE
    slots = {}
    if tiles > 1:
        scaled = values[:whole, column : column + width].astype(jnp.float32)
        scaled = (scaled * dot(coefs[:whole, :], hot[near])).astype(jnp.bfloat16)
    held = [None] * near
    for b in range(tiles - 1):
        now = dot(keys[here(b), :], scaled[here(b), :], ((0,), (0,)))
        for k in range(near):
            if not (b >> k) & 1:
                held[k] = now
                slots[k, b >> k] = now.astype(jnp.bfloat16)
                break
            since = sum(totals[(b >> k) << k : b + 1])
            now = now + held[k] * head_row(jnp.exp(since)[:, :1], width, head_dim)

    for b in range(tiles):
        sums = all_sums[b * heads : (b + 1) * heads]
        scores = dot(queries[here(b), :], keys[here(b), :], ((1,), (1,)))
        scores = jnp.where(causal, scores, 0.0)
        block = values[here(b), column : column + width]
        mixed = []
        for part in range(width // LANES):
            values_here = block[:, part * LANES : (part + 1) * LANES]
            left, right = [], []
            for inner in range(per_tile):
                head = part * per_tile + inner
                own = jnp.broadcast_to(columns[b][:, head : head + 1], (TILE, TILE))
                beside = columns[b][SPAN:, heads + head : heads + head + 1]
                below = jnp.where(early, jnp.broadcast_to(beside, (SPAN, TILE)), own[SPAN:])
                gap = jnp.concatenate([own[:SPAN], below], axis=0) - sums[head : head + 1, :]
                left.append((jnp.exp(jnp.minimum(gap, 80.0)) * scores).astype(jnp.bfloat16))
                right.append(jnp.where(lane_head == inner, values_here, jnp.zeros_like(values_here)))
            mixed.append(dot(jnp.concatenate(left, axis=1), jnp.concatenate(right, axis=0)))
        for at in range(0, width, WIDE):
            lanes = slice(at, min(at + WIDE, width))
            total = jnp.concatenate(mixed[at // LANES : (at + WIDE) // LANES], axis=1)
            for k in range(near):
                if (b >> k) & 1:
                    reached = dot(queries[here(b), :], slots[k, (b >> k) - 1][:, lanes])
                    total += dot(coefs[here(b), :], hot[k][:, lanes]) * reached
            out[here(b), lanes] = total


def gate_kernel(
    head_dim, heads, first, column, xor, far, four, arrivals, me, *refs
):
    local, coefs, queries, gate, *rest = refs
    got = [rest[sum(arrivals[:m]) : sum(arrivals[: m + 1])] for m in range(len(arrivals))]
    at = sum(arrivals)
    befores = 0 if four else far
    before, outs = rest[at : at + befores], rest[at + befores :]
    count = len(outs) if xor else outs[0].shape[0]
    rows = local.shape[0] // count
    width = local.shape[1]
    states = queries.shape[1]
    hot = [spread(first + m * heads, width, head_dim) for m in range(far)]
    arrived = []
    if four:
        near_by, next_by, over = (part[...].astype(jnp.float32) for (part,) in got)
        decays = next_by[states : states + SUBLANES] + next_by[states + SUBLANES :]
        last = jnp.where(lax.axis_index("seq") == 3, 1.0, 0.0)
        arrived.append(near_by[:states] + next_by[:states] * last)
        arrived.append(next_by[:states] * (1.0 - last) + over[:states] * decays[:1])
        arrived = [state.astype(jnp.bfloat16) for state in arrived]
    else:
        for m in range(far):
            state = sum(part[:states, :].astype(jnp.float32) for part in got[m])
            arrived.append((state * before[m][:1]).astype(jnp.bfloat16))

    def fill(place, out):
        here = pl.ds(pl.multiple_of(place * rows, rows), rows)
        for at in range(0, width, WIDE):
            end = min(at + WIDE, width)
            total = local[here, at:end]
            for m in range(far):
                reached = dot(queries[here, :], arrived[m][:, at:end])
                total += dot(coefs[here, :], hot[m][:, at:end]) * reached
            opened = 0.5 * gate[here, column + at : column + end].astype(jnp.float32)
            out[:, at:end] = (total * opened * (1.0 + jnp.tanh(opened))).astype(jnp.bfloat16)

    if xor:
        for index, out in enumerate(outs):
            fill(jnp.bitwise_xor(me[0], index), out)
    else:

        @pl.loop(0, count)
        def _(index):
            fill(index, outs[0].at[index])


def norm_kernel(sources, xor, me, gain, *rest):
    parts, (out, done, sent) = rest[:-3], rest[-3:]
    rows, group_width = done.shape[1:]
    some = min(rows, 4 * SUBLANES)
    copies = []
    for index, places in enumerate(sources):
        group = jnp.bitwise_xor(me[0], index) if xor else index
        columns = pl.ds(pl.multiple_of(group * group_width, group_width), group_width)
        for top in range(0, rows, some):
            here = slice(top, top + some)
            blocks = [parts[n][here, :] if at is None else parts[n][at, here, :] for n, at in places]
            blocks = [block.astype(jnp.float32) for block in blocks]
            square = sum(jnp.sum(block * block, axis=1, keepdims=True) for block in blocks)
            scale = lax.rsqrt(square / group_width + 1e-05)
            normed = jnp.concatenate([block * scale for block in blocks], axis=1)
            done[index, here, :] = (normed * gain[:, columns]).astype(out.dtype)
        copies.append(pltpu.make_async_copy(done.at[index], out.at[:, columns], sent.at[index]))
        copies[-1].start()
    for copy in copies:
        copy.wait()


def partners(count):
    return sorted(range(1, count), key=lambda apart: (-apart.bit_count(), -apart))


def params(limit):
    return pltpu.CompilerParams(vmem_limit_bytes=limit * MIB)


def body(values, gate_z, b_keys, c_queries, log_decay, level_weight, doc_start, norm_gain):
    tokens, width = values.shape
    heads_here = log_decay.shape[1]
    head_dim = width // heads_here
    state_size = b_keys.shape[2]
    tiles = tokens // TILE
    near = tiles.bit_length() - 1
    seq_count = lax.axis_size("seq")
    far = seq_count.bit_length() - 1
    head_count = lax.axis_size("head")
    head_index = lax.axis_index("head")
    group_index = head_index * heads_here // (MIXER_HEADS // GROUPS)
    key_rows = lax.dynamic_index_in_dim(b_keys, group_index, 1, keepdims=False)
    query_rows = lax.dynamic_index_in_dim(c_queries, group_index, 1, keepdims=False)
    decay = jnp.transpose(log_decay)
    weight = jnp.transpose(level_weight, (2, 1, 0))
    heads = SUBLANES
    if heads_here < heads:
        short = heads - heads_here
        decay = jnp.pad(decay, ((0, short), (0, 0)))
        weight = jnp.pad(weight, ((0, 0), (0, short), (0, 0)), constant_values=1.0)
    chunks = max(1, heads_here // heads)
    part = width // chunks
    levels = weight.shape[0]
    smem = pl.BlockSpec(memory_space=pltpu.SMEM)

    whole = pl.BlockSpec(memory_space=pltpu.VMEM)
    anywhere = pl.BlockSpec(memory_space=pl.ANY)
    far_away = pl.BlockSpec(memory_space=pltpu.HBM)

    def state_call(c):
        pieces = min(4, tiles)
        return pl.pallas_call(
            functools.partial(state_kernel, head_dim, c, pieces),
            in_specs=[far_away, far_away, whole, far_away, anywhere],
            out_specs=[whole, whole, whole],
            out_shape=[
                jax.ShapeDtypeStruct((state_size, part), jnp.float32),
                jax.ShapeDtypeStruct((state_size + 2 * SUBLANES, part), jnp.bfloat16),
                jax.ShapeDtypeStruct((SUBLANES, part), jnp.float32),
            ],
            scratch_shapes=[
                pltpu.SMEM(doc_start.shape, doc_start.dtype),
                pltpu.VMEM((heads, tokens), jnp.float32),
                pltpu.VMEM((tokens, part), jnp.bfloat16),
                pltpu.SemaphoreType.DMA((pieces + 2,)),
            ],
            compiler_params=params(16),
            cost_estimate=pl.CostEstimate(
                flops=4 * tokens * state_size * part, bytes_accessed=3 * tokens * part, transcendentals=0
            ),
            name="block_state",
        )(doc_start, decay, key_rows, values, key_rows if c == 0 else query_rows)

    def local_call(c, follow):
        return pl.pallas_call(
            functools.partial(local_kernel, head_dim, heads, c, far),
            in_specs=[smem] + [whole] * 5 + [anywhere] * len(follow),
            out_specs=[whole] * 2,
            out_shape=[
                jax.ShapeDtypeStruct((tokens, part), jnp.float32),
                jax.ShapeDtypeStruct((tokens, 2 * LANES), jnp.bfloat16),
            ],
            compiler_params=params(16),
            cost_estimate=pl.CostEstimate(
                flops=16 * tokens * state_size * part, bytes_accessed=12 * tokens * part, transcendentals=0
            ),
            name="local_mixer",
        )(doc_start, decay, weight, values, query_rows, key_rows, *follow)

    rows = tokens // head_count
    direct = head_count == GROUPS
    me = jnp.reshape(head_index, (1,)).astype(jnp.int32)

    def gate_call(c, local, coefs, chain):
        if direct:
            out_shape = [jax.ShapeDtypeStruct((rows, part), jnp.bfloat16)] * head_count
        else:
            out_shape = [jax.ShapeDtypeStruct((head_count, rows, part), jnp.bfloat16)]
        states = [one for got, _ in chain.arrived for one in got]
        if not four:
            states += [before for _, before in chain.arrived]
        arrivals = [len(got) for got, _ in chain.arrived]
        return pl.pallas_call(
            functools.partial(
                gate_kernel,
                head_dim,
                heads,
                (near + 3) * heads,
                c * part,
                direct,
                far,
                four,
                arrivals,
            ),
            in_specs=[smem] + [whole] * (4 + len(states)),
            out_specs=[whole] * len(out_shape),
            out_shape=out_shape,
            compiler_params=params(16),
            cost_estimate=pl.CostEstimate(
                flops=4 * tokens * state_size * part, bytes_accessed=8 * tokens * part, transcendentals=0
            ),
            name="far_and_gate",
        )(me, local, coefs, query_rows, gate_z, *states)

    def merge_call(bit, got, own, through, before, follow):
        return pl.pallas_call(
            functools.partial(merge_kernel, bit, len(got)),
            in_specs=[anywhere] + [whole] * (len(got) + 3),
            out_specs=[whole] * 4,
            out_shape=[
                jax.ShapeDtypeStruct(own.shape, jnp.float32),
                jax.ShapeDtypeStruct(through.shape, jnp.float32),
                jax.ShapeDtypeStruct(through.shape, jnp.float32),
                jax.ShapeDtypeStruct(got[0].shape, jnp.bfloat16),
            ],
            compiler_params=params(4),
            cost_estimate=pl.CostEstimate(
                flops=8 * state_size * part, bytes_accessed=16 * state_size * part, transcendentals=0
            ),
            name="merge_blocks",
        )(follow, *got, own, through, before)

    four = seq_count == 4
    if four:
        phases = [[[(0, 1)]], [[(1, 2), (2, 3)], [(1, 3)]]]
    else:
        phases = []
        for size in (2**bit for bit in range(far)):
            source = range(size - 1, seq_count, 2 * size)
            phases.append([[(s, s + up) for s in source] for up in range(1, size + 1)])

    class Chain:
        def __init__(self, c):
            self.own, self.moving, self.through = state_call(c)
            self.before = jnp.ones_like(self.through)
            self.arrived = []

        def post(self):
            got = [lax.ppermute(self.moving, "seq", p) for p in phases[len(self.arrived)]]
            self.arrived.append((got, self.before))

        def finish(self, follow):
            while self.arrived and len(self.arrived) < far:
                got = self.arrived[-1][0]
                bit = len(self.arrived) - 1
                self.own, self.through, self.before, self.moving = merge_call(
                    bit, got, self.own, self.through, self.before, follow
                )
                self.post()
            if four and len(self.arrived) == far:
                self.arrived = [([one], None) for got, _ in self.arrived for one in got]

    chains = [Chain(c) for c in range(chunks)]
    if far:
        for chain in chains:
            chain.post()
    for chain in chains:
        chain.finish(key_rows)
    pieces = []
    follow = [chains[-1].moving]
    for c in range(chunks):
        if c:
            follow = follow + [one for got, _ in chains[c].arrived for one in got]
        local, coefs = local_call(c, follow)
        out = gate_call(c, local, coefs, chains[c])
        follow = [out[0]]
        if direct:
            got = [out[0]] + [None] * (head_count - 1)
            for apart in partners(head_count):
                pairs = [(source, source ^ apart) for source in range(head_count)]
                got[apart] = lax.ppermute(out[apart], "head", pairs)
            pieces.append(got)
        else:
            pieces.append(lax.all_to_all(out[0], "head", split_axis=0, concat_axis=0))

    gain = jnp.reshape(norm_gain, (1, -1))
    group_width = width * head_count // GROUPS

    if direct:
        operands = [piece for got in pieces for piece in got]
        sources = [[(c * head_count + k, None) for c in range(chunks)] for k in range(head_count)]
    else:
        operands = pieces
        per_group = group_width // width
        sources = [
            [(c, g * per_group + n) for n in range(per_group) for c in range(chunks)]
            for g in range(GROUPS)
        ]
    return pl.pallas_call(
        functools.partial(norm_kernel, sources, direct),
        in_specs=[smem, whole] + [whole] * len(operands),
        out_specs=far_away,
        out_shape=jax.ShapeDtypeStruct((rows, width * head_count), jnp.bfloat16),
        scratch_shapes=[
            pltpu.VMEM((GROUPS, rows, group_width), jnp.bfloat16),
            pltpu.SemaphoreType.DMA((GROUPS,)),
        ],
        compiler_params=params(16),
        cost_estimate=pl.CostEstimate(
            flops=8 * tokens * width, bytes_accessed=4 * tokens * width, transcendentals=0
        ),
        name="norm_rows",
    )(me, gain, *operands)


def solution(mesh):
    in_specs = (
        P("seq", "head"),
        P("seq", "head"),
        P("seq", None, None),
        P("seq", None, None),
        P("seq", "head"),
        P("seq", "head", None),
        P(),
        P(),
    )
    out_specs = P(("seq", "head"), None)
    return jax.shard_map(body, mesh=mesh, in_specs=in_specs, out_specs=out_specs, check_vma=False)
```

```python
import functools

import jax
import jax.numpy as jnp
from jax import lax
from jax.experimental import pallas as pl
from jax.experimental.pallas import tpu as pltpu
from jax.sharding import PartitionSpec as P

MIXER_HEADS = 128
GROUPS = 8
SPAN = 64
TILE = 2 * SPAN
LANES = 128
WIDE = 2 * LANES
SUBLANES = 8
NEVER = -1e30
HIGHEST = lax.Precision.HIGHEST
MIB = 2**20


def dot(left, right, contract=((1,), (0,)), precision=None):
    return lax.dot_general(
        left, right, (contract, ((), ())), precision=precision, preferred_element_type=jnp.float32
    )


def iota(shape, axis):
    return lax.broadcasted_iota(jnp.int32, shape, axis)


def halves(coef):
    high = coef.astype(jnp.bfloat16)
    low = (coef - high.astype(jnp.float32)).astype(jnp.bfloat16)
    return jnp.concatenate([high, low], axis=1)


def spread(first, width, head_dim):
    row = jnp.bitwise_and(iota((2 * LANES, width), 0), LANES - 1)
    head = jnp.right_shift(iota((2 * LANES, width), 1), head_dim.bit_length() - 1)
    return jnp.where(row == head + first, 1.0, 0.0).astype(jnp.bfloat16)


def head_row(column, width, head_dim):
    shape = (column.shape[0], width)
    head = jnp.right_shift(iota(shape, 1), head_dim.bit_length() - 1)
    return jnp.sum(jnp.where(head == iota(shape, 0), column, 0.0), axis=0, keepdims=True)


def stack_rows(pieces):
    rows = sum(piece.shape[0] for piece in pieces)
    if rows < LANES:
        pieces = pieces + [jnp.zeros((LANES - rows, LANES), jnp.float32)]
    return jnp.transpose(jnp.concatenate(pieces, axis=0))


def tile_rows(decay):
    tiles = decay.shape[1] // TILE
    return jnp.concatenate([decay[:, b * TILE : (b + 1) * TILE] for b in range(tiles)], axis=0)


def resets(docs, tiles):
    first = lax.axis_index("seq") * (tiles * (TILE // SPAN))
    shut = [NEVER * docs[first + s].astype(jnp.float32) for s in range(tiles * (TILE // SPAN))]
    return [shut[2 * b : 2 * b + 2] for b in range(tiles)]


def pack(total, through):
    high = through.astype(jnp.bfloat16)
    low = (through - high.astype(jnp.float32)).astype(jnp.bfloat16)
    return jnp.concatenate([total.astype(jnp.bfloat16), high, low], axis=0)


def decay_kernel(head_dim, heads, docs, decay, *outs):
    chunks = len(outs) // 2
    tiles = decay.shape[1] // TILE
    shut = resets(docs, tiles)
    lane = iota((heads, TILE), 1)
    later = jnp.where(iota((TILE, TILE), 0) > iota((TILE, TILE), 1), 1.0, 0.0)
    for c in range(chunks):
        terms, through = outs[2 * c : 2 * c + 2]
        stacked = tile_rows(decay[c * heads : (c + 1) * heads, :])
        suffix = dot(stacked, later, precision=HIGHEST)
        totals = jnp.sum(stacked, axis=1, keepdims=True)
        after = jnp.zeros((heads, 1), jnp.float32)
        closed = jnp.float32(0.0)
        scales = [None] * tiles
        for b in reversed(range(tiles)):
            ends = jnp.where(lane < SPAN, closed + shut[b][1], closed)
            scales[b] = jnp.exp(suffix[b * heads : (b + 1) * heads] + after + ends)
            closed = closed + shut[b][1] + shut[b][0]
            after = after + totals[b * heads : (b + 1) * heads]
        terms[...] = halves(stack_rows(scales))
        row = head_row(jnp.exp(after + closed), through.shape[1], head_dim)
        through[...] = jnp.broadcast_to(row, through.shape)


def state_kernel(
    head_dim, heads, column, pieces, terms, through, keys, values, follow, state, message
):
    del follow
    width = state.shape[1]
    tokens = keys.shape[0]
    tiles = tokens // TILE
    rows = tokens // pieces
    owner = jnp.right_shift(
        jnp.bitwise_and(iota((1, 2 * LANES), 1), LANES - 1), heads.bit_length() - 1
    )
    shape = (2 * LANES, width)
    same = jnp.bitwise_and(iota(shape, 0), heads - 1) == jnp.right_shift(
        iota(shape, 1), head_dim.bit_length() - 1
    )
    one_hot = jnp.where(same, 1.0, 0.0).astype(jnp.bfloat16)
    chosen = [
        terms[...] * jnp.where(owner == b, 1.0, 0.0).astype(jnp.bfloat16) for b in range(tiles)
    ]
    total = jnp.zeros(state.shape, jnp.float32)
    for i in range(pieces):
        span = tiles // pieces
        here = slice(i * rows, (i + 1) * rows)
        scale = dot(jnp.concatenate(chosen[i * span : (i + 1) * span], axis=0), one_hot)
        scaled = values[here, column : column + width].astype(jnp.float32) * scale
        total += dot(keys[here, :], scaled.astype(jnp.bfloat16), ((0,), (0,)))
    state[...] = total
    message[...] = pack(total, through[...])


def merge_kernel(bit, arrivals, follow, *refs):
    del follow
    got, (own, through, before, new_own, new_through, new_before, message) = (
        refs[:arrivals],
        refs[arrivals:],
    )
    states = own.shape[0]
    total = sum(part[...].astype(jnp.float32) for part in got)
    decays = total[states : states + SUBLANES] + total[states + SUBLANES :]
    upper = jnp.bitwise_and(jnp.right_shift(lax.axis_index("seq"), bit), 1).astype(jnp.float32)
    new_before[...] = before[...] * (decays + (1.0 - upper))
    summed = own[...] + total[:states] * through[:1]
    passed = through[...] * (decays + (1.0 - upper))
    new_own[...] = summed
    new_through[...] = passed
    message[...] = pack(summed, passed)


def local_kernel(
    head_dim, heads, chunk, far, docs, decay, weight, values, queries, keys, *rest
):
    out, coefs = rest[-2:]
    tokens, width = out.shape
    column = chunk * width
    mine = slice(chunk * heads, (chunk + 1) * heads)
    tiles = tokens // TILE
    near = tiles.bit_length() - 1
    shut = resets(docs, tiles)
    lane = iota((heads, TILE), 1)
    upto = jnp.where(iota((TILE, TILE), 0) <= iota((TILE, TILE), 1), 1.0, 0.0)
    all_sums = dot(tile_rows(decay[mine, :]), upto, precision=HIGHEST)
    causal = iota((TILE, TILE), 0) >= iota((TILE, TILE), 1)
    early = iota((SPAN, TILE), 1) < SPAN
    per_tile = LANES // head_dim
    lane_head = jnp.right_shift(iota((TILE, LANES), 1), head_dim.bit_length() - 1)
    hot = [spread((2 + i) * heads, width, head_dim) for i in range(near + 1)]

    def here(b):
        return slice(b * TILE, (b + 1) * TILE)

    columns, totals = [], []
    for b in range(tiles):
        sums = all_sums[b * heads : (b + 1) * heads]
        scale = [weight[level, mine, here(b)] for level in range(weight.shape[0])]
        last = jnp.broadcast_to(sums[:, TILE - 1 :], sums.shape)
        opened = sums + jnp.where(lane < SPAN, shut[b][0], shut[b][0] + shut[b][1])
        rows = [sums + jnp.log(scale[0]), sums + jnp.log(scale[1]) + shut[b][1]]
        for k in range(near):
            if (b >> k) & 1:
                since = sum(totals[(b >> k) << k : b], jnp.zeros_like(sums))
                rows.append(jnp.exp(opened + since) * scale[2 + k])
            else:
                rows.append(jnp.zeros_like(sums))
        rows.append(jnp.exp(last - sums + jnp.where(lane < SPAN, shut[b][1], 0.0)))
        since = sum(totals, jnp.zeros_like(sums))
        rows += [jnp.exp(opened + since) * scale[2 + near + m] for m in range(far)]
        totals.append(last + (shut[b][0] + shut[b][1]))
        columns.append(stack_rows(rows))
        coefs[here(b), :] = halves(columns[b])

    whole = (tiles - 1) * TILE
    slots = {}
    if tiles > 1:
        scaled = values[:whole, column : column + width].astype(jnp.float32)
        scaled = (scaled * dot(coefs[:whole, :], hot[near])).astype(jnp.bfloat16)
    held = [None] * near
    for b in range(tiles - 1):
        now = dot(keys[here(b), :], scaled[here(b), :], ((0,), (0,)))
        for k in range(near):
            if not (b >> k) & 1:
                held[k] = now
                slots[k, b >> k] = now.astype(jnp.bfloat16)
                break
            since = sum(totals[(b >> k) << k : b + 1])
            now = now + held[k] * head_row(jnp.exp(since)[:, :1], width, head_dim)

    for b in range(tiles):
        sums = all_sums[b * heads : (b + 1) * heads]
        scores = dot(queries[here(b), :], keys[here(b), :], ((1,), (1,)))
        scores = jnp.where(causal, scores, 0.0)
        block = values[here(b), column : column + width]
        mixed = []
        for part in range(width // LANES):
            values_here = block[:, part * LANES : (part + 1) * LANES]
            left, right = [], []
            for inner in range(per_tile):
                head = part * per_tile + inner
                own = jnp.broadcast_to(columns[b][:, head : head + 1], (TILE, TILE))
                beside = columns[b][SPAN:, heads + head : heads + head + 1]
                below = jnp.where(early, jnp.broadcast_to(beside, (SPAN, TILE)), own[SPAN:])
                gap = jnp.concatenate([own[:SPAN], below], axis=0) - sums[head : head + 1, :]
                left.append((jnp.exp(jnp.minimum(gap, 80.0)) * scores).astype(jnp.bfloat16))
                right.append(jnp.where(lane_head == inner, values_here, jnp.zeros_like(values_here)))
            mixed.append(dot(jnp.concatenate(left, axis=1), jnp.concatenate(right, axis=0)))
        for at in range(0, width, WIDE):
            lanes = slice(at, min(at + WIDE, width))
            total = jnp.concatenate(mixed[at // LANES : (at + WIDE) // LANES], axis=1)
            for k in range(near):
                if (b >> k) & 1:
                    reached = dot(queries[here(b), :], slots[k, (b >> k) - 1][:, lanes])
                    total += dot(coefs[here(b), :], hot[k][:, lanes]) * reached
            out[here(b), lanes] = total


def gate_kernel(
    head_dim, heads, first, column, xor, far, four, arrivals, joined, me, *refs
):
    local, coefs, queries, gate, *rest = refs
    got = [rest[sum(arrivals[:m]) : sum(arrivals[: m + 1])] for m in range(len(arrivals))]
    at = sum(arrivals)
    befores = 0 if four else far
    before, rest = rest[at : at + befores], rest[at + befores :]
    earlier, outs = rest[: sum(joined.values())], rest[sum(joined.values()) :]
    count = len(outs) if xor else outs[0].shape[0]
    rows = local.shape[0] // count
    width = local.shape[1]
    states = queries.shape[1]
    hot = [spread(first + m * heads, width, head_dim) for m in range(far)]
    arrived = []
    if four:
        near_by, next_by, over = (part[...].astype(jnp.float32) for (part,) in got)
        decays = next_by[states : states + SUBLANES] + next_by[states + SUBLANES :]
        last = jnp.where(lax.axis_index("seq") == 3, 1.0, 0.0)
        arrived.append(near_by[:states] + next_by[:states] * last)
        arrived.append(next_by[:states] * (1.0 - last) + over[:states] * decays[:1])
        arrived = [state.astype(jnp.bfloat16) for state in arrived]
    else:
        for m in range(far):
            state = sum(part[:states, :].astype(jnp.float32) for part in got[m])
            arrived.append((state * before[m][:1]).astype(jnp.bfloat16))

    def fill(place, out):
        here = pl.ds(pl.multiple_of(place * rows, rows), rows)
        for at in range(0, width, WIDE):
            end = min(at + WIDE, width)
            total = local[here, at:end]
            for m in range(far):
                reached = dot(queries[here, :], arrived[m][:, at:end])
                total += dot(coefs[here, :], hot[m][:, at:end]) * reached
            opened = 0.5 * gate[here, column + at : column + end].astype(jnp.float32)
            out[:, at:end] = (total * opened * (1.0 + jnp.tanh(opened))).astype(jnp.bfloat16)

    if xor:
        at = 0
        for index, out in enumerate(outs):
            prior = joined.get(index, 0) * width
            for start in range(0, prior, width):
                out[:, start : start + width] = earlier[at][...]
                at += 1
            fill(jnp.bitwise_xor(me[0], index), out.at[:, prior : prior + width])
    else:

        @pl.loop(0, count)
        def _(index):
            fill(index, outs[0].at[index])


def norm_kernel(sources, xor, me, gain, *rest):
    parts, (out, done, sent) = rest[:-3], rest[-3:]
    rows, group_width = done.shape[1:]
    some = min(rows, 4 * SUBLANES)
    copies = []
    for index, places in enumerate(sources):
        group = jnp.bitwise_xor(me[0], index) if xor else index
        columns = pl.ds(pl.multiple_of(group * group_width, group_width), group_width)
        for top in range(0, rows, some):
            here = slice(top, top + some)
            blocks = [parts[n][here, :] if at is None else parts[n][at, here, :] for n, at in places]
            blocks = [block.astype(jnp.float32) for block in blocks]
            square = sum(jnp.sum(block * block, axis=1, keepdims=True) for block in blocks)
            scale = lax.rsqrt(square / group_width + 1e-05)
            normed = jnp.concatenate([block * scale for block in blocks], axis=1)
            done[index, here, :] = (normed * gain[:, columns]).astype(out.dtype)
        copies.append(pltpu.make_async_copy(done.at[index], out.at[:, columns], sent.at[index]))
        copies[-1].start()
    for copy in copies:
        copy.wait()


def partners(count, final):
    if final:
        return sorted(range(1, count), key=lambda apart: (apart in (1, 4), apart != 5, -apart))
    return sorted(range(1, count), key=lambda apart: (-apart.bit_count(), -apart))


def params(limit):
    return pltpu.CompilerParams(vmem_limit_bytes=limit * MIB)


def body(values, gate_z, b_keys, c_queries, log_decay, level_weight, doc_start, norm_gain):
    tokens, width = values.shape
    heads_here = log_decay.shape[1]
    head_dim = width // heads_here
    state_size = b_keys.shape[2]
    tiles = tokens // TILE
    near = tiles.bit_length() - 1
    seq_count = lax.axis_size("seq")
    far = seq_count.bit_length() - 1
    head_count = lax.axis_size("head")
    head_index = lax.axis_index("head")
    group_index = head_index * heads_here // (MIXER_HEADS // GROUPS)
    key_rows = lax.dynamic_index_in_dim(b_keys, group_index, 1, keepdims=False)
    query_rows = lax.dynamic_index_in_dim(c_queries, group_index, 1, keepdims=False)
    decay = jnp.transpose(log_decay)
    weight = jnp.transpose(level_weight, (2, 1, 0))
    heads = SUBLANES
    if heads_here < heads:
        short = heads - heads_here
        decay = jnp.pad(decay, ((0, short), (0, 0)))
        weight = jnp.pad(weight, ((0, 0), (0, short), (0, 0)), constant_values=1.0)
    chunks = max(1, heads_here // heads)
    part = width // chunks
    levels = weight.shape[0]
    smem = pl.BlockSpec(memory_space=pltpu.SMEM)

    whole = pl.BlockSpec(memory_space=pltpu.VMEM)
    anywhere = pl.BlockSpec(memory_space=pl.ANY)
    far_away = pl.BlockSpec(memory_space=pltpu.HBM)

    decays = pl.pallas_call(
        functools.partial(decay_kernel, head_dim, heads),
        in_specs=[smem, whole],
        out_specs=[whole] * (2 * chunks),
        out_shape=[
            jax.ShapeDtypeStruct((LANES, 2 * LANES), jnp.bfloat16),
            jax.ShapeDtypeStruct((SUBLANES, part), jnp.float32),
        ]
        * chunks,
        compiler_params=params(8),
        cost_estimate=pl.CostEstimate(
            flops=tokens * width, bytes_accessed=4 * tokens * part, transcendentals=0
        ),
        name="token_decays",
    )(doc_start, decay)

    def state_call(c):
        terms, through = decays[2 * c : 2 * c + 2]
        pieces = min(4, tiles)
        state, message = pl.pallas_call(
            functools.partial(state_kernel, head_dim, heads, c * part, pieces),
            in_specs=[whole, whole, whole, whole, anywhere],
            out_specs=[whole, whole],
            out_shape=[
                jax.ShapeDtypeStruct((state_size, part), jnp.float32),
                jax.ShapeDtypeStruct((state_size + 2 * SUBLANES, part), jnp.bfloat16),
            ],
            compiler_params=params(16),
            cost_estimate=pl.CostEstimate(
                flops=4 * tokens * state_size * part, bytes_accessed=3 * tokens * part, transcendentals=0
            ),
            name="block_state",
        )(terms, through, key_rows, values, key_rows if c == 0 else query_rows)
        return state, message, through

    def local_call(c, follow):
        return pl.pallas_call(
            functools.partial(local_kernel, head_dim, heads, c, far),
            in_specs=[smem] + [whole] * 5 + [anywhere] * len(follow),
            out_specs=[whole] * 2,
            out_shape=[
                jax.ShapeDtypeStruct((tokens, part), jnp.float32),
                jax.ShapeDtypeStruct((tokens, 2 * LANES), jnp.bfloat16),
            ],
            compiler_params=params(16),
            cost_estimate=pl.CostEstimate(
                flops=16 * tokens * state_size * part, bytes_accessed=12 * tokens * part, transcendentals=0
            ),
            name="local_mixer",
        )(doc_start, decay, weight, values, query_rows, key_rows, *follow)

    rows = tokens // head_count
    direct = head_count == GROUPS
    me = jnp.reshape(head_index, (1,)).astype(jnp.int32)

    def gate_call(c, local, coefs, chain, earlier):
        joined = {apart: len(kept) for apart, kept in earlier.items()}
        if direct:
            out_shape = [
                jax.ShapeDtypeStruct((rows, part * (1 + joined.get(k, 0))), jnp.bfloat16)
                for k in range(head_count)
            ]
        else:
            out_shape = [jax.ShapeDtypeStruct((head_count, rows, part), jnp.bfloat16)]
        states = [one for got, _ in chain.arrived for one in got]
        if not four:
            states += [before for _, before in chain.arrived]
        arrivals = [len(got) for got, _ in chain.arrived]
        states += [one for apart in sorted(earlier) for one in earlier[apart]]
        return pl.pallas_call(
            functools.partial(
                gate_kernel,
                head_dim,
                heads,
                (near + 3) * heads,
                c * part,
                direct,
                far,
                four,
                arrivals,
                joined,
            ),
            in_specs=[smem] + [whole] * (4 + len(states)),
            out_specs=[whole] * len(out_shape),
            out_shape=out_shape,
            compiler_params=params(16),
            cost_estimate=pl.CostEstimate(
                flops=4 * tokens * state_size * part, bytes_accessed=8 * tokens * part, transcendentals=0
            ),
            name="far_and_gate",
        )(me, local, coefs, query_rows, gate_z, *states)

    def merge_call(bit, got, own, through, before, follow):
        return pl.pallas_call(
            functools.partial(merge_kernel, bit, len(got)),
            in_specs=[anywhere] + [whole] * (len(got) + 3),
            out_specs=[whole] * 4,
            out_shape=[
                jax.ShapeDtypeStruct(own.shape, jnp.float32),
                jax.ShapeDtypeStruct(through.shape, jnp.float32),
                jax.ShapeDtypeStruct(through.shape, jnp.float32),
                jax.ShapeDtypeStruct(got[0].shape, jnp.bfloat16),
            ],
            compiler_params=params(4),
            cost_estimate=pl.CostEstimate(
                flops=8 * state_size * part, bytes_accessed=16 * state_size * part, transcendentals=0
            ),
            name="merge_blocks",
        )(follow, *got, own, through, before)

    four = seq_count == 4
    if four:
        phases = [[[(0, 1)]], [[(1, 2), (2, 3)], [(1, 3)]]]
    else:
        phases = []
        for size in (2**bit for bit in range(far)):
            source = range(size - 1, seq_count, 2 * size)
            phases.append([[(s, s + up) for s in source] for up in range(1, size + 1)])

    class Chain:
        def __init__(self, c):
            self.own, self.moving, self.through = state_call(c)
            self.before = jnp.ones_like(self.through)
            self.arrived = []

        def post(self):
            got = [lax.ppermute(self.moving, "seq", p) for p in phases[len(self.arrived)]]
            self.arrived.append((got, self.before))

        def finish(self, follow):
            while self.arrived and len(self.arrived) < far:
                got = self.arrived[-1][0]
                bit = len(self.arrived) - 1
                self.own, self.through, self.before, self.moving = merge_call(
                    bit, got, self.own, self.through, self.before, follow
                )
                self.post()
            if four and len(self.arrived) == far:
                self.arrived = [([one], None) for got, _ in self.arrived for one in got]

    chains = [Chain(c) for c in range(chunks)]
    if far:
        for chain in chains:
            chain.post()
    for chain in chains:
        chain.finish(key_rows)
    held = (1, 2)
    kept = {}
    pieces = []
    follow = [chains[-1].moving]
    for c in range(chunks):
        if c:
            follow = follow + [one for got, _ in chains[c].arrived for one in got]
        local, coefs = local_call(c, follow)
        final = c + 1 == chunks
        out = gate_call(c, local, coefs, chains[c], kept if final else {})
        follow = [out[0]]
        if direct:
            got = [out[0]] + [None] * (head_count - 1)
            for apart in partners(head_count, final):
                if not final and apart in held:
                    kept.setdefault(apart, []).append(out[apart])
                    continue
                pairs = [(source, source ^ apart) for source in range(head_count)]
                got[apart] = lax.ppermute(out[apart], "head", pairs)
            pieces.append(got)
        else:
            pieces.append(lax.all_to_all(out[0], "head", split_axis=0, concat_axis=0))

    gain = jnp.reshape(norm_gain, (1, -1))
    group_width = width * head_count // GROUPS

    if direct:
        operands, sources = [], []
        for k in range(head_count):
            mine = [got[k] for got in pieces if got[k] is not None]
            sources.append([(len(operands) + n, None) for n in range(len(mine))])
            operands += mine
    else:
        operands = pieces
        per_group = group_width // width
        sources = [
            [(c, g * per_group + n) for n in range(per_group) for c in range(chunks)]
            for g in range(GROUPS)
        ]
    return pl.pallas_call(
        functools.partial(norm_kernel, sources, direct),
        in_specs=[smem, whole] + [whole] * len(operands),
        out_specs=far_away,
        out_shape=jax.ShapeDtypeStruct((rows, width * head_count), jnp.bfloat16),
        scratch_shapes=[
            pltpu.VMEM((GROUPS, rows, group_width), jnp.bfloat16),
            pltpu.SemaphoreType.DMA((GROUPS,)),
        ],
        compiler_params=params(16),
        cost_estimate=pl.CostEstimate(
            flops=8 * tokens * width, bytes_accessed=4 * tokens * width, transcendentals=0
        ),
        name="norm_rows",
    )(me, gain, *operands)


def solution(mesh):
    in_specs = (
        P("seq", "head"),
        P("seq", "head"),
        P("seq", None, None),
        P("seq", None, None),
        P("seq", "head"),
        P("seq", "head", None),
        P(),
        P(),
    )
    out_specs = P(("seq", "head"), None)
    return jax.shard_map(body, mesh=mesh, in_specs=in_specs, out_specs=out_specs, check_vma=False)
```

```python
import functools

import jax
import jax.numpy as jnp
from jax import lax
from jax.experimental import pallas as pl
from jax.experimental.pallas import tpu as pltpu
from jax.sharding import PartitionSpec as P

MIXER_HEADS = 128
GROUPS = 8
SPAN = 64
TILE = 2 * SPAN
LANES = 128
WIDE = 2 * LANES
SUBLANES = 8
NEVER = -1e30
HIGHEST = lax.Precision.HIGHEST
MIB = 2**20


def dot(left, right, contract=((1,), (0,)), precision=None):
    return lax.dot_general(
        left, right, (contract, ((), ())), precision=precision, preferred_element_type=jnp.float32
    )


def iota(shape, axis):
    return lax.broadcasted_iota(jnp.int32, shape, axis)


def halves(coef):
    high = coef.astype(jnp.bfloat16)
    low = (coef - high.astype(jnp.float32)).astype(jnp.bfloat16)
    return jnp.concatenate([high, low], axis=1)


def spread(first, width, head_dim):
    row = jnp.bitwise_and(iota((2 * LANES, width), 0), LANES - 1)
    head = jnp.right_shift(iota((2 * LANES, width), 1), head_dim.bit_length() - 1)
    return jnp.where(row == head + first, 1.0, 0.0).astype(jnp.bfloat16)


def head_row(column, width, head_dim):
    shape = (column.shape[0], width)
    head = jnp.right_shift(iota(shape, 1), head_dim.bit_length() - 1)
    return jnp.sum(jnp.where(head == iota(shape, 0), column, 0.0), axis=0, keepdims=True)


def stack_rows(pieces):
    rows = sum(piece.shape[0] for piece in pieces)
    if rows < LANES:
        pieces = pieces + [jnp.zeros((LANES - rows, LANES), jnp.float32)]
    return jnp.transpose(jnp.concatenate(pieces, axis=0))


def tile_rows(decay):
    tiles = decay.shape[1] // TILE
    return jnp.concatenate([decay[:, b * TILE : (b + 1) * TILE] for b in range(tiles)], axis=0)


def resets(docs, tiles):
    first = lax.axis_index("seq") * (tiles * (TILE // SPAN))
    shut = [NEVER * docs[first + s].astype(jnp.float32) for s in range(tiles * (TILE // SPAN))]
    return [shut[2 * b : 2 * b + 2] for b in range(tiles)]


def pack(total, through):
    high = through.astype(jnp.bfloat16)
    low = (through - high.astype(jnp.float32)).astype(jnp.bfloat16)
    return jnp.concatenate([total.astype(jnp.bfloat16), high, low], axis=0)


def decay_kernel(head_dim, heads, docs, decay, *outs):
    chunks = len(outs) // 2
    tiles = decay.shape[1] // TILE
    shut = resets(docs, tiles)
    lane = iota((heads, TILE), 1)
    later = jnp.where(iota((TILE, TILE), 0) > iota((TILE, TILE), 1), 1.0, 0.0)
    for c in range(chunks):
        terms, through = outs[2 * c : 2 * c + 2]
        stacked = tile_rows(decay[c * heads : (c + 1) * heads, :])
        suffix = dot(stacked, later, precision=HIGHEST)
        totals = jnp.sum(stacked, axis=1, keepdims=True)
        after = jnp.zeros((heads, 1), jnp.float32)
        closed = jnp.float32(0.0)
        scales = [None] * tiles
        for b in reversed(range(tiles)):
            ends = jnp.where(lane < SPAN, closed + shut[b][1], closed)
            scales[b] = jnp.exp(suffix[b * heads : (b + 1) * heads] + after + ends)
            closed = closed + shut[b][1] + shut[b][0]
            after = after + totals[b * heads : (b + 1) * heads]
        terms[...] = halves(stack_rows(scales))
        row = head_row(jnp.exp(after + closed), through.shape[1], head_dim)
        through[...] = jnp.broadcast_to(row, through.shape)


def state_kernel(
    head_dim, heads, column, pieces, terms, through, keys, values, follow, state, message
):
    del follow
    width = state.shape[1]
    tokens = keys.shape[0]
    tiles = tokens // TILE
    rows = tokens // pieces
    owner = jnp.right_shift(
        jnp.bitwise_and(iota((1, 2 * LANES), 1), LANES - 1), heads.bit_length() - 1
    )
    shape = (2 * LANES, width)
    same = jnp.bitwise_and(iota(shape, 0), heads - 1) == jnp.right_shift(
        iota(shape, 1), head_dim.bit_length() - 1
    )
    one_hot = jnp.where(same, 1.0, 0.0).astype(jnp.bfloat16)
    chosen = [
        terms[...] * jnp.where(owner == b, 1.0, 0.0).astype(jnp.bfloat16) for b in range(tiles)
    ]
    total = jnp.zeros(state.shape, jnp.float32)
    for i in range(pieces):
        span = tiles // pieces
        here = slice(i * rows, (i + 1) * rows)
        scale = dot(jnp.concatenate(chosen[i * span : (i + 1) * span], axis=0), one_hot)
        scaled = values[here, column : column + width].astype(jnp.float32) * scale
        total += dot(keys[here, :], scaled.astype(jnp.bfloat16), ((0,), (0,)))
    state[...] = total
    message[...] = pack(total, through[...])


def merge_kernel(bit, arrivals, follow, *refs):
    del follow
    got, (own, through, before, new_own, new_through, new_before, message) = (
        refs[:arrivals],
        refs[arrivals:],
    )
    states = own.shape[0]
    total = sum(part[...].astype(jnp.float32) for part in got)
    decays = total[states : states + SUBLANES] + total[states + SUBLANES :]
    upper = jnp.bitwise_and(jnp.right_shift(lax.axis_index("seq"), bit), 1).astype(jnp.float32)
    new_before[...] = before[...] * (decays + (1.0 - upper))
    summed = own[...] + total[:states] * through[:1]
    passed = through[...] * (decays + (1.0 - upper))
    new_own[...] = summed
    new_through[...] = passed
    message[...] = pack(summed, passed)


def local_kernel(
    head_dim, heads, chunk, far, docs, decay, weight, values, queries, keys, *rest
):
    out, coefs = rest[-2:]
    tokens, width = out.shape
    column = chunk * width
    mine = slice(chunk * heads, (chunk + 1) * heads)
    tiles = tokens // TILE
    near = tiles.bit_length() - 1
    shut = resets(docs, tiles)
    lane = iota((heads, TILE), 1)
    upto = jnp.where(iota((TILE, TILE), 0) <= iota((TILE, TILE), 1), 1.0, 0.0)
    all_sums = dot(tile_rows(decay[mine, :]), upto, precision=HIGHEST)
    causal = iota((TILE, TILE), 0) >= iota((TILE, TILE), 1)
    early = iota((SPAN, TILE), 1) < SPAN
    per_tile = LANES // head_dim
    lane_head = jnp.right_shift(iota((TILE, LANES), 1), head_dim.bit_length() - 1)
    hot = [spread((2 + i) * heads, width, head_dim) for i in range(near + 1)]

    def here(b):
        return slice(b * TILE, (b + 1) * TILE)

    columns, totals = [], []
    for b in range(tiles):
        sums = all_sums[b * heads : (b + 1) * heads]
        scale = [weight[level, mine, here(b)] for level in range(weight.shape[0])]
        last = jnp.broadcast_to(sums[:, TILE - 1 :], sums.shape)
        opened = sums + jnp.where(lane < SPAN, shut[b][0], shut[b][0] + shut[b][1])
        rows = [sums + jnp.log(scale[0]), sums + jnp.log(scale[1]) + shut[b][1]]
        for k in range(near):
            if (b >> k) & 1:
                since = sum(totals[(b >> k) << k : b], jnp.zeros_like(sums))
                rows.append(jnp.exp(opened + since) * scale[2 + k])
            else:
                rows.append(jnp.zeros_like(sums))
        rows.append(jnp.exp(last - sums + jnp.where(lane < SPAN, shut[b][1], 0.0)))
        since = sum(totals, jnp.zeros_like(sums))
        rows += [jnp.exp(opened + since) * scale[2 + near + m] for m in range(far)]
        totals.append(last + (shut[b][0] + shut[b][1]))
        columns.append(stack_rows(rows))
        coefs[here(b), :] = halves(columns[b])

    whole = (tiles - 1) * TILE
    slots = {}
    if tiles > 1:
        scaled = values[:whole, column : column + width].astype(jnp.float32)
        scaled = (scaled * dot(coefs[:whole, :], hot[near])).astype(jnp.bfloat16)
    held = [None] * near
    for b in range(tiles - 1):
        now = dot(keys[here(b), :], scaled[here(b), :], ((0,), (0,)))
        for k in range(near):
            if not (b >> k) & 1:
                held[k] = now
                slots[k, b >> k] = now.astype(jnp.bfloat16)
                break
            since = sum(totals[(b >> k) << k : b + 1])
            now = now + held[k] * head_row(jnp.exp(since)[:, :1], width, head_dim)

    for b in range(tiles):
        sums = all_sums[b * heads : (b + 1) * heads]
        scores = dot(queries[here(b), :], keys[here(b), :], ((1,), (1,)))
        scores = jnp.where(causal, scores, 0.0)
        block = values[here(b), column : column + width]
        mixed = []
        for part in range(width // LANES):
            values_here = block[:, part * LANES : (part + 1) * LANES]
            left, right = [], []
            for inner in range(per_tile):
                head = part * per_tile + inner
                own = jnp.broadcast_to(columns[b][:, head : head + 1], (TILE, TILE))
                beside = columns[b][SPAN:, heads + head : heads + head + 1]
                below = jnp.where(early, jnp.broadcast_to(beside, (SPAN, TILE)), own[SPAN:])
                gap = jnp.concatenate([own[:SPAN], below], axis=0) - sums[head : head + 1, :]
                left.append((jnp.exp(jnp.minimum(gap, 80.0)) * scores).astype(jnp.bfloat16))
                right.append(jnp.where(lane_head == inner, values_here, jnp.zeros_like(values_here)))
            mixed.append(dot(jnp.concatenate(left, axis=1), jnp.concatenate(right, axis=0)))
        for at in range(0, width, WIDE):
            lanes = slice(at, min(at + WIDE, width))
            total = jnp.concatenate(mixed[at // LANES : (at + WIDE) // LANES], axis=1)
            for k in range(near):
                if (b >> k) & 1:
                    reached = dot(queries[here(b), :], slots[k, (b >> k) - 1][:, lanes])
                    total += dot(coefs[here(b), :], hot[k][:, lanes]) * reached
            out[here(b), lanes] = total


def gate_kernel(
    head_dim, heads, first, column, xor, far, four, arrivals, joined, me, *refs
):
    local, coefs, queries, gate, *rest = refs
    got = [rest[sum(arrivals[:m]) : sum(arrivals[: m + 1])] for m in range(len(arrivals))]
    at = sum(arrivals)
    befores = 0 if four else far
    before, rest = rest[at : at + befores], rest[at + befores :]
    earlier, outs = rest[: sum(joined.values())], rest[sum(joined.values()) :]
    count = len(outs) if xor else outs[0].shape[0]
    rows = local.shape[0] // count
    width = local.shape[1]
    states = queries.shape[1]
    hot = [spread(first + m * heads, width, head_dim) for m in range(far)]
    arrived = []
    if four:
        near_by, next_by, over = (part[...].astype(jnp.float32) for (part,) in got)
        decays = next_by[states : states + SUBLANES] + next_by[states + SUBLANES :]
        last = jnp.where(lax.axis_index("seq") == 3, 1.0, 0.0)
        arrived.append(near_by[:states] + next_by[:states] * last)
        arrived.append(next_by[:states] * (1.0 - last) + over[:states] * decays[:1])
        arrived = [state.astype(jnp.bfloat16) for state in arrived]
    else:
        for m in range(far):
            state = sum(part[:states, :].astype(jnp.float32) for part in got[m])
            arrived.append((state * before[m][:1]).astype(jnp.bfloat16))

    def fill(place, out):
        here = pl.ds(pl.multiple_of(place * rows, rows), rows)
        for at in range(0, width, WIDE):
            end = min(at + WIDE, width)
            total = local[here, at:end]
            for m in range(far):
                reached = dot(queries[here, :], arrived[m][:, at:end])
                total += dot(coefs[here, :], hot[m][:, at:end]) * reached
            opened = 0.5 * gate[here, column + at : column + end].astype(jnp.float32)
            out[:, at:end] = (total * opened * (1.0 + jnp.tanh(opened))).astype(jnp.bfloat16)

    if xor:
        at = 0
        for index, out in enumerate(outs):
            prior = joined.get(index, 0) * width
            for start in range(0, prior, width):
                out[:, start : start + width] = earlier[at][...]
                at += 1
            fill(jnp.bitwise_xor(me[0], index), out.at[:, prior : prior + width])
    else:

        @pl.loop(0, count)
        def _(index):
            fill(index, outs[0].at[index])


def norm_kernel(sources, xor, me, gain, *rest):
    parts, (out, done, sent) = rest[:-3], rest[-3:]
    rows, group_width = done.shape[1:]
    some = min(rows, 4 * SUBLANES)
    copies = []
    for index, places in enumerate(sources):
        group = jnp.bitwise_xor(me[0], index) if xor else index
        columns = pl.ds(pl.multiple_of(group * group_width, group_width), group_width)
        for top in range(0, rows, some):
            here = slice(top, top + some)
            blocks = [parts[n][here, :] if at is None else parts[n][at, here, :] for n, at in places]
            blocks = [block.astype(jnp.float32) for block in blocks]
            square = sum(jnp.sum(block * block, axis=1, keepdims=True) for block in blocks)
            scale = lax.rsqrt(square / group_width + 1e-05)
            normed = jnp.concatenate([block * scale for block in blocks], axis=1)
            done[index, here, :] = (normed * gain[:, columns]).astype(out.dtype)
        copies.append(pltpu.make_async_copy(done.at[index], out.at[:, columns], sent.at[index]))
        copies[-1].start()
    for copy in copies:
        copy.wait()


def partners(count, final):
    if final:
        return sorted(range(1, count), key=lambda apart: (apart in (1, 4), apart != 5, -apart))
    return sorted(range(1, count), key=lambda apart: (-apart.bit_count(), -apart))


def params(limit):
    return pltpu.CompilerParams(vmem_limit_bytes=limit * MIB)


def body(values, gate_z, b_keys, c_queries, log_decay, level_weight, doc_start, norm_gain):
    tokens, width = values.shape
    heads_here = log_decay.shape[1]
    head_dim = width // heads_here
    state_size = b_keys.shape[2]
    tiles = tokens // TILE
    near = tiles.bit_length() - 1
    seq_count = lax.axis_size("seq")
    far = seq_count.bit_length() - 1
    head_count = lax.axis_size("head")
    head_index = lax.axis_index("head")
    group_index = head_index * heads_here // (MIXER_HEADS // GROUPS)
    decay = jnp.transpose(log_decay)
    weight = jnp.transpose(level_weight, (2, 1, 0))
    heads = SUBLANES
    if heads_here < heads:
        short = heads - heads_here
        decay = jnp.pad(decay, ((0, short), (0, 0)))
        weight = jnp.pad(weight, ((0, 0), (0, short), (0, 0)), constant_values=1.0)
    chunks = max(1, heads_here // heads)
    part = width // chunks
    levels = weight.shape[0]
    smem = pl.BlockSpec(memory_space=pltpu.SMEM)

    whole = pl.BlockSpec(memory_space=pltpu.VMEM)
    anywhere = pl.BlockSpec(memory_space=pl.ANY)
    far_away = pl.BlockSpec(memory_space=pltpu.HBM)

    decays = pl.pallas_call(
        functools.partial(decay_kernel, head_dim, heads),
        in_specs=[smem, whole],
        out_specs=[whole] * (2 * chunks),
        out_shape=[
            jax.ShapeDtypeStruct((LANES, 2 * LANES), jnp.bfloat16),
            jax.ShapeDtypeStruct((SUBLANES, part), jnp.float32),
        ]
        * chunks,
        compiler_params=params(8),
        cost_estimate=pl.CostEstimate(
            flops=tokens * width, bytes_accessed=4 * tokens * part, transcendentals=0
        ),
        name="token_decays",
    )(doc_start, decay)

    group_index, _ = lax.optimization_barrier((group_index, decays[1]))
    key_rows = lax.dynamic_index_in_dim(b_keys, group_index, 1, keepdims=False)
    query_rows = lax.dynamic_index_in_dim(c_queries, group_index, 1, keepdims=False)

    def state_call(c):
        terms, through = decays[2 * c : 2 * c + 2]
        pieces = min(4, tiles)
        state, message = pl.pallas_call(
            functools.partial(state_kernel, head_dim, heads, c * part, pieces),
            in_specs=[whole, whole, whole, whole, anywhere],
            out_specs=[whole, whole],
            out_shape=[
                jax.ShapeDtypeStruct((state_size, part), jnp.float32),
                jax.ShapeDtypeStruct((state_size + 2 * SUBLANES, part), jnp.bfloat16),
            ],
            compiler_params=params(16),
            cost_estimate=pl.CostEstimate(
                flops=4 * tokens * state_size * part, bytes_accessed=3 * tokens * part, transcendentals=0
            ),
            name="block_state",
        )(terms, through, key_rows, values, key_rows if c == 0 else query_rows)
        return state, message, through

    def local_call(c, follow):
        return pl.pallas_call(
            functools.partial(local_kernel, head_dim, heads, c, far),
            in_specs=[smem] + [whole] * 5 + [anywhere] * len(follow),
            out_specs=[whole] * 2,
            out_shape=[
                jax.ShapeDtypeStruct((tokens, part), jnp.float32),
                jax.ShapeDtypeStruct((tokens, 2 * LANES), jnp.bfloat16),
            ],
            compiler_params=params(16),
            cost_estimate=pl.CostEstimate(
                flops=16 * tokens * state_size * part, bytes_accessed=12 * tokens * part, transcendentals=0
            ),
            name="local_mixer",
        )(doc_start, decay, weight, values, query_rows, key_rows, *follow)

    rows = tokens // head_count
    direct = head_count == GROUPS
    me = jnp.reshape(head_index, (1,)).astype(jnp.int32)

    def gate_call(c, local, coefs, chain, earlier):
        joined = {apart: len(kept) for apart, kept in earlier.items()}
        if direct:
            out_shape = [
                jax.ShapeDtypeStruct((rows, part * (1 + joined.get(k, 0))), jnp.bfloat16)
                for k in range(head_count)
            ]
        else:
            out_shape = [jax.ShapeDtypeStruct((head_count, rows, part), jnp.bfloat16)]
        states = [one for got, _ in chain.arrived for one in got]
        if not four:
            states += [before for _, before in chain.arrived]
        arrivals = [len(got) for got, _ in chain.arrived]
        states += [one for apart in sorted(earlier) for one in earlier[apart]]
        return pl.pallas_call(
            functools.partial(
                gate_kernel,
                head_dim,
                heads,
                (near + 3) * heads,
                c * part,
                direct,
                far,
                four,
                arrivals,
                joined,
            ),
            in_specs=[smem] + [whole] * (4 + len(states)),
            out_specs=[whole] * len(out_shape),
            out_shape=out_shape,
            compiler_params=params(16),
            cost_estimate=pl.CostEstimate(
                flops=4 * tokens * state_size * part, bytes_accessed=8 * tokens * part, transcendentals=0
            ),
            name="far_and_gate",
        )(me, local, coefs, query_rows, gate_z, *states)

    def merge_call(bit, got, own, through, before, follow):
        return pl.pallas_call(
            functools.partial(merge_kernel, bit, len(got)),
            in_specs=[anywhere] + [whole] * (len(got) + 3),
            out_specs=[whole] * 4,
            out_shape=[
                jax.ShapeDtypeStruct(own.shape, jnp.float32),
                jax.ShapeDtypeStruct(through.shape, jnp.float32),
                jax.ShapeDtypeStruct(through.shape, jnp.float32),
                jax.ShapeDtypeStruct(got[0].shape, jnp.bfloat16),
            ],
            compiler_params=params(4),
            cost_estimate=pl.CostEstimate(
                flops=8 * state_size * part, bytes_accessed=16 * state_size * part, transcendentals=0
            ),
            name="merge_blocks",
        )(follow, *got, own, through, before)

    four = seq_count == 4
    if four:
        phases = [[[(0, 1)]], [[(1, 2), (2, 3)], [(1, 3)]]]
    else:
        phases = []
        for size in (2**bit for bit in range(far)):
            source = range(size - 1, seq_count, 2 * size)
            phases.append([[(s, s + up) for s in source] for up in range(1, size + 1)])

    class Chain:
        def __init__(self, c):
            self.own, self.moving, self.through = state_call(c)
            self.before = jnp.ones_like(self.through)
            self.arrived = []

        def post(self):
            got = [lax.ppermute(self.moving, "seq", p) for p in phases[len(self.arrived)]]
            self.arrived.append((got, self.before))

        def finish(self, follow):
            while self.arrived and len(self.arrived) < far:
                got = self.arrived[-1][0]
                bit = len(self.arrived) - 1
                self.own, self.through, self.before, self.moving = merge_call(
                    bit, got, self.own, self.through, self.before, follow
                )
                self.post()
            if four and len(self.arrived) == far:
                self.arrived = [([one], None) for got, _ in self.arrived for one in got]

    chains = [Chain(c) for c in range(chunks)]
    if far:
        for chain in chains:
            chain.post()
    for chain in chains:
        chain.finish(key_rows)
    held = (1, 2)
    kept = {}
    pieces = []
    follow = [chains[-1].moving]
    for c in range(chunks):
        if c:
            follow = follow + [one for got, _ in chains[c].arrived for one in got]
        local, coefs = local_call(c, follow)
        final = c + 1 == chunks
        out = gate_call(c, local, coefs, chains[c], kept if final else {})
        follow = [out[0]]
        if direct:
            got = [out[0]] + [None] * (head_count - 1)
            for apart in partners(head_count, final):
                if not final and apart in held:
                    kept.setdefault(apart, []).append(out[apart])
                    continue
                pairs = [(source, source ^ apart) for source in range(head_count)]
                got[apart] = lax.ppermute(out[apart], "head", pairs)
            pieces.append(got)
        else:
            pieces.append(lax.all_to_all(out[0], "head", split_axis=0, concat_axis=0))

    gain = jnp.reshape(norm_gain, (1, -1))
    group_width = width * head_count // GROUPS

    if direct:
        operands, sources = [], []
        for k in range(head_count):
            mine = [got[k] for got in pieces if got[k] is not None]
            sources.append([(len(operands) + n, None) for n in range(len(mine))])
            operands += mine
    else:
        operands = pieces
        per_group = group_width // width
        sources = [
            [(c, g * per_group + n) for n in range(per_group) for c in range(chunks)]
            for g in range(GROUPS)
        ]
    return pl.pallas_call(
        functools.partial(norm_kernel, sources, direct),
        in_specs=[smem, whole] + [whole] * len(operands),
        out_specs=far_away,
        out_shape=jax.ShapeDtypeStruct((rows, width * head_count), jnp.bfloat16),
        scratch_shapes=[
            pltpu.VMEM((GROUPS, rows, group_width), jnp.bfloat16),
            pltpu.SemaphoreType.DMA((GROUPS,)),
        ],
        compiler_params=params(16),
        cost_estimate=pl.CostEstimate(
            flops=8 * tokens * width, bytes_accessed=4 * tokens * width, transcendentals=0
        ),
        name="norm_rows",
    )(me, gain, *operands)


def solution(mesh):
    in_specs = (
        P("seq", "head"),
        P("seq", "head"),
        P("seq", None, None),
        P("seq", None, None),
        P("seq", "head"),
        P("seq", "head", None),
        P(),
        P(),
    )
    out_specs = P(("seq", "head"), None)
    return jax.shard_map(body, mesh=mesh, in_specs=in_specs, out_specs=out_specs, check_vma=False)
```

```python
import functools

import jax
import jax.numpy as jnp
from jax import lax
from jax.experimental import pallas as pl
from jax.experimental.pallas import tpu as pltpu
from jax.sharding import PartitionSpec as P

MIXER_HEADS = 128
GROUPS = 8
SPAN = 64
TILE = 2 * SPAN
LANES = 128
WIDE = 2 * LANES
SUBLANES = 8
NEVER = -1e30
HIGHEST = lax.Precision.HIGHEST
MIB = 2**20


def dot(left, right, contract=((1,), (0,)), precision=None):
    return lax.dot_general(
        left, right, (contract, ((), ())), precision=precision, preferred_element_type=jnp.float32
    )


def iota(shape, axis):
    return lax.broadcasted_iota(jnp.int32, shape, axis)


def halves(coef):
    high = coef.astype(jnp.bfloat16)
    low = (coef - high.astype(jnp.float32)).astype(jnp.bfloat16)
    return jnp.concatenate([high, low], axis=1)


def spread(first, width, head_dim):
    row = jnp.bitwise_and(iota((2 * LANES, width), 0), LANES - 1)
    head = jnp.right_shift(iota((2 * LANES, width), 1), head_dim.bit_length() - 1)
    return jnp.where(row == head + first, 1.0, 0.0).astype(jnp.bfloat16)


def head_row(column, width, head_dim):
    shape = (column.shape[0], width)
    head = jnp.right_shift(iota(shape, 1), head_dim.bit_length() - 1)
    return jnp.sum(jnp.where(head == iota(shape, 0), column, 0.0), axis=0, keepdims=True)


def stack_rows(pieces):
    rows = sum(piece.shape[0] for piece in pieces)
    if rows < LANES:
        pieces = pieces + [jnp.zeros((LANES - rows, LANES), jnp.float32)]
    return jnp.transpose(jnp.concatenate(pieces, axis=0))


def tile_rows(decay):
    tiles = decay.shape[1] // TILE
    return jnp.concatenate([decay[:, b * TILE : (b + 1) * TILE] for b in range(tiles)], axis=0)


def resets(docs, tiles):
    first = lax.axis_index("seq") * (tiles * (TILE // SPAN))
    shut = [NEVER * docs[first + s].astype(jnp.float32) for s in range(tiles * (TILE // SPAN))]
    return [shut[2 * b : 2 * b + 2] for b in range(tiles)]


def pack(total, through):
    high = through.astype(jnp.bfloat16)
    low = (through - high.astype(jnp.float32)).astype(jnp.bfloat16)
    return jnp.concatenate([total.astype(jnp.bfloat16), high, low], axis=0)


def decay_kernel(head_dim, heads, docs, decay, *outs):
    chunks = len(outs) // 2
    tiles = decay.shape[1] // TILE
    shut = resets(docs, tiles)
    lane = iota((heads, TILE), 1)
    later = jnp.where(iota((TILE, TILE), 0) > iota((TILE, TILE), 1), 1.0, 0.0)
    for c in range(chunks):
        terms, through = outs[2 * c : 2 * c + 2]
        stacked = tile_rows(decay[c * heads : (c + 1) * heads, :])
        suffix = dot(stacked, later, precision=HIGHEST)
        totals = jnp.sum(stacked, axis=1, keepdims=True)
        after = jnp.zeros((heads, 1), jnp.float32)
        closed = jnp.float32(0.0)
        scales = [None] * tiles
        for b in reversed(range(tiles)):
            ends = jnp.where(lane < SPAN, closed + shut[b][1], closed)
            scales[b] = jnp.exp(suffix[b * heads : (b + 1) * heads] + after + ends)
            closed = closed + shut[b][1] + shut[b][0]
            after = after + totals[b * heads : (b + 1) * heads]
        terms[...] = halves(stack_rows(scales))
        row = head_row(jnp.exp(after + closed), through.shape[1], head_dim)
        through[...] = jnp.broadcast_to(row, through.shape)


def state_kernel(
    head_dim, heads, column, pieces, terms, through, keys, values, follow, state, message
):
    del follow
    width = state.shape[1]
    tokens = keys.shape[0]
    tiles = tokens // TILE
    rows = tokens // pieces
    owner = jnp.right_shift(
        jnp.bitwise_and(iota((1, 2 * LANES), 1), LANES - 1), heads.bit_length() - 1
    )
    shape = (2 * LANES, width)
    same = jnp.bitwise_and(iota(shape, 0), heads - 1) == jnp.right_shift(
        iota(shape, 1), head_dim.bit_length() - 1
    )
    one_hot = jnp.where(same, 1.0, 0.0).astype(jnp.bfloat16)
    chosen = [
        terms[...] * jnp.where(owner == b, 1.0, 0.0).astype(jnp.bfloat16) for b in range(tiles)
    ]
    total = jnp.zeros(state.shape, jnp.float32)
    for i in range(pieces):
        span = tiles // pieces
        here = slice(i * rows, (i + 1) * rows)
        scale = dot(jnp.concatenate(chosen[i * span : (i + 1) * span], axis=0), one_hot)
        scaled = values[here, column : column + width].astype(jnp.float32) * scale
        total += dot(keys[here, :], scaled.astype(jnp.bfloat16), ((0,), (0,)))
    state[...] = total
    message[...] = pack(total, through[...])


def merge_kernel(bit, arrivals, *refs):
    got, (own, through, before, message, *new) = refs[:arrivals], refs[arrivals:]
    states = own.shape[0]
    total = sum(part[...].astype(jnp.float32) for part in got)
    decays = total[states : states + SUBLANES] + total[states + SUBLANES :]
    upper = jnp.bitwise_and(jnp.right_shift(lax.axis_index("seq"), bit), 1).astype(jnp.float32)
    summed = own[...] + total[:states] * through[:1]
    passed = through[...] * (decays + (1.0 - upper))
    message[...] = pack(summed, passed)
    if new:
        new_own, new_through, new_before = new
        new_before[...] = before[...] * (decays + (1.0 - upper))
        new_own[...] = summed
        new_through[...] = passed


def local_kernel(
    head_dim, heads, chunk, far, docs, decay, weight, values, queries, keys, *rest
):
    out, coefs = rest[-2:]
    tokens, width = out.shape
    column = chunk * width
    mine = slice(chunk * heads, (chunk + 1) * heads)
    tiles = tokens // TILE
    near = tiles.bit_length() - 1
    shut = resets(docs, tiles)
    lane = iota((heads, TILE), 1)
    upto = jnp.where(iota((TILE, TILE), 0) <= iota((TILE, TILE), 1), 1.0, 0.0)
    all_sums = dot(tile_rows(decay[mine, :]), upto, precision=HIGHEST)
    causal = iota((TILE, TILE), 0) >= iota((TILE, TILE), 1)
    early = iota((SPAN, TILE), 1) < SPAN
    per_tile = LANES // head_dim
    lane_head = jnp.right_shift(iota((TILE, LANES), 1), head_dim.bit_length() - 1)
    hot = [spread((2 + i) * heads, width, head_dim) for i in range(near + 1)]

    def here(b):
        return slice(b * TILE, (b + 1) * TILE)

    columns, totals = [], []
    for b in range(tiles):
        sums = all_sums[b * heads : (b + 1) * heads]
        scale = [weight[level, mine, here(b)] for level in range(weight.shape[0])]
        last = jnp.broadcast_to(sums[:, TILE - 1 :], sums.shape)
        opened = sums + jnp.where(lane < SPAN, shut[b][0], shut[b][0] + shut[b][1])
        rows = [sums + jnp.log(scale[0]), sums + jnp.log(scale[1]) + shut[b][1]]
        for k in range(near):
            if (b >> k) & 1:
                since = sum(totals[(b >> k) << k : b], jnp.zeros_like(sums))
                rows.append(jnp.exp(opened + since) * scale[2 + k])
            else:
                rows.append(jnp.zeros_like(sums))
        rows.append(jnp.exp(last - sums + jnp.where(lane < SPAN, shut[b][1], 0.0)))
        since = sum(totals, jnp.zeros_like(sums))
        rows += [jnp.exp(opened + since) * scale[2 + near + m] for m in range(far)]
        totals.append(last + (shut[b][0] + shut[b][1]))
        columns.append(stack_rows(rows))
        coefs[here(b), :] = halves(columns[b])

    whole = (tiles - 1) * TILE
    slots = {}
    if tiles > 1:
        scaled = values[:whole, column : column + width].astype(jnp.float32)
        scaled = (scaled * dot(coefs[:whole, :], hot[near])).astype(jnp.bfloat16)
    held = [None] * near
    for b in range(tiles - 1):
        now = dot(keys[here(b), :], scaled[here(b), :], ((0,), (0,)))
        for k in range(near):
            if not (b >> k) & 1:
                held[k] = now
                slots[k, b >> k] = now.astype(jnp.bfloat16)
                break
            since = sum(totals[(b >> k) << k : b + 1])
            now = now + held[k] * head_row(jnp.exp(since)[:, :1], width, head_dim)

    for b in range(tiles):
        sums = all_sums[b * heads : (b + 1) * heads]
        scores = dot(queries[here(b), :], keys[here(b), :], ((1,), (1,)))
        scores = jnp.where(causal, scores, 0.0)
        block = values[here(b), column : column + width]
        mixed = []
        for part in range(width // LANES):
            values_here = block[:, part * LANES : (part + 1) * LANES]
            left, right = [], []
            for inner in range(per_tile):
                head = part * per_tile + inner
                own = jnp.broadcast_to(columns[b][:, head : head + 1], (TILE, TILE))
                beside = columns[b][SPAN:, heads + head : heads + head + 1]
                below = jnp.where(early, jnp.broadcast_to(beside, (SPAN, TILE)), own[SPAN:])
                gap = jnp.concatenate([own[:SPAN], below], axis=0) - sums[head : head + 1, :]
                left.append((jnp.exp(jnp.minimum(gap, 80.0)) * scores).astype(jnp.bfloat16))
                right.append(jnp.where(lane_head == inner, values_here, jnp.zeros_like(values_here)))
            mixed.append(dot(jnp.concatenate(left, axis=1), jnp.concatenate(right, axis=0)))
        for at in range(0, width, WIDE):
            lanes = slice(at, min(at + WIDE, width))
            total = jnp.concatenate(mixed[at // LANES : (at + WIDE) // LANES], axis=1)
            for k in range(near):
                if (b >> k) & 1:
                    reached = dot(queries[here(b), :], slots[k, (b >> k) - 1][:, lanes])
                    total += dot(coefs[here(b), :], hot[k][:, lanes]) * reached
            out[here(b), lanes] = total


def gate_kernel(
    head_dim, heads, first, column, xor, far, four, arrivals, joined, me, *refs
):
    local, coefs, queries, gate, *rest = refs
    got = [rest[sum(arrivals[:m]) : sum(arrivals[: m + 1])] for m in range(len(arrivals))]
    at = sum(arrivals)
    befores = 0 if four else far
    before, rest = rest[at : at + befores], rest[at + befores :]
    earlier, outs = rest[: sum(joined.values())], rest[sum(joined.values()) :]
    count = len(outs) if xor else outs[0].shape[0]
    rows = local.shape[0] // count
    width = local.shape[1]
    states = queries.shape[1]
    hot = [spread(first + m * heads, width, head_dim) for m in range(far)]
    arrived = []
    if four:
        near_by, next_by, over = (part[...].astype(jnp.float32) for (part,) in got)
        decays = next_by[states : states + SUBLANES] + next_by[states + SUBLANES :]
        last = jnp.where(lax.axis_index("seq") == 3, 1.0, 0.0)
        arrived.append(near_by[:states] + next_by[:states] * last)
        arrived.append(next_by[:states] * (1.0 - last) + over[:states] * decays[:1])
        arrived = [state.astype(jnp.bfloat16) for state in arrived]
    else:
        for m in range(far):
            state = sum(part[:states, :].astype(jnp.float32) for part in got[m])
            arrived.append((state * before[m][:1]).astype(jnp.bfloat16))

    def fill(place, out):
        here = pl.ds(pl.multiple_of(place * rows, rows), rows)
        for at in range(0, width, WIDE):
            end = min(at + WIDE, width)
            total = local[here, at:end]
            for m in range(far):
                reached = dot(queries[here, :], arrived[m][:, at:end])
                total += dot(coefs[here, :], hot[m][:, at:end]) * reached
            opened = 0.5 * gate[here, column + at : column + end].astype(jnp.float32)
            out[:, at:end] = (total * opened * (1.0 + jnp.tanh(opened))).astype(jnp.bfloat16)

    if xor:
        at = 0
        for index, out in enumerate(outs):
            prior = joined.get(index, 0) * width
            for start in range(0, prior, width):
                out[:, start : start + width] = earlier[at][...]
                at += 1
            fill(jnp.bitwise_xor(me[0], index), out.at[:, prior : prior + width])
    else:

        @pl.loop(0, count)
        def _(index):
            fill(index, outs[0].at[index])


def norm_kernel(sources, xor, me, gain, *rest):
    parts, (out, done, sent) = rest[:-3], rest[-3:]
    rows, group_width = done.shape[1:]
    some = min(rows, 4 * SUBLANES)
    copies = []
    for index, places in enumerate(sources):
        group = jnp.bitwise_xor(me[0], index) if xor else index
        columns = pl.ds(pl.multiple_of(group * group_width, group_width), group_width)
        for top in range(0, rows, some):
            here = slice(top, top + some)
            blocks = [parts[n][here, :] if at is None else parts[n][at, here, :] for n, at in places]
            blocks = [block.astype(jnp.float32) for block in blocks]
            square = sum(jnp.sum(block * block, axis=1, keepdims=True) for block in blocks)
            scale = lax.rsqrt(square / group_width + 1e-05)
            normed = jnp.concatenate([block * scale for block in blocks], axis=1)
            done[index, here, :] = (normed * gain[:, columns]).astype(out.dtype)
        copies.append(pltpu.make_async_copy(done.at[index], out.at[:, columns], sent.at[index]))
        copies[-1].start()
    for copy in copies:
        copy.wait()


def partners(count, final):
    if final:
        return sorted(range(1, count), key=lambda apart: (apart in (1, 4), apart != 5, -apart))
    return sorted(range(1, count), key=lambda apart: (-apart.bit_count(), -apart))


def params(limit):
    return pltpu.CompilerParams(vmem_limit_bytes=limit * MIB)


def body(values, gate_z, b_keys, c_queries, log_decay, level_weight, doc_start, norm_gain):
    tokens, width = values.shape
    heads_here = log_decay.shape[1]
    head_dim = width // heads_here
    state_size = b_keys.shape[2]
    tiles = tokens // TILE
    near = tiles.bit_length() - 1
    seq_count = lax.axis_size("seq")
    far = seq_count.bit_length() - 1
    head_count = lax.axis_size("head")
    head_index = lax.axis_index("head")
    group_index = head_index * heads_here // (MIXER_HEADS // GROUPS)
    decay = jnp.transpose(log_decay)
    weight = jnp.transpose(level_weight, (2, 1, 0))
    heads = SUBLANES
    if heads_here < heads:
        short = heads - heads_here
        decay = jnp.pad(decay, ((0, short), (0, 0)))
        weight = jnp.pad(weight, ((0, 0), (0, short), (0, 0)), constant_values=1.0)
    chunks = max(1, heads_here // heads)
    part = width // chunks
    levels = weight.shape[0]
    smem = pl.BlockSpec(memory_space=pltpu.SMEM)

    whole = pl.BlockSpec(memory_space=pltpu.VMEM)
    anywhere = pl.BlockSpec(memory_space=pl.ANY)
    far_away = pl.BlockSpec(memory_space=pltpu.HBM)

    decays = pl.pallas_call(
        functools.partial(decay_kernel, head_dim, heads),
        in_specs=[smem, whole],
        out_specs=[whole] * (2 * chunks),
        out_shape=[
            jax.ShapeDtypeStruct((LANES, 2 * LANES), jnp.bfloat16),
            jax.ShapeDtypeStruct((SUBLANES, part), jnp.float32),
        ]
        * chunks,
        compiler_params=params(8),
        cost_estimate=pl.CostEstimate(
            flops=tokens * width, bytes_accessed=4 * tokens * part, transcendentals=0
        ),
        name="token_decays",
    )(doc_start, decay)

    group_index, _ = lax.optimization_barrier((group_index, decays[1]))
    key_rows = lax.dynamic_index_in_dim(b_keys, group_index, 1, keepdims=False)
    query_rows = lax.dynamic_index_in_dim(c_queries, group_index, 1, keepdims=False)

    def state_call(c):
        terms, through = decays[2 * c : 2 * c + 2]
        pieces = min(4, tiles)
        state, message = pl.pallas_call(
            functools.partial(state_kernel, head_dim, heads, c * part, pieces),
            in_specs=[whole, whole, whole, whole, anywhere],
            out_specs=[whole, whole],
            out_shape=[
                jax.ShapeDtypeStruct((state_size, part), jnp.float32),
                jax.ShapeDtypeStruct((state_size + 2 * SUBLANES, part), jnp.bfloat16),
            ],
            compiler_params=params(16),
            cost_estimate=pl.CostEstimate(
                flops=4 * tokens * state_size * part, bytes_accessed=3 * tokens * part, transcendentals=0
            ),
            name="block_state",
        )(terms, through, key_rows, values, key_rows if c == 0 else query_rows)
        return state, message, through

    def local_call(c, follow):
        return pl.pallas_call(
            functools.partial(local_kernel, head_dim, heads, c, far),
            in_specs=[smem] + [whole] * 5 + [anywhere] * len(follow),
            out_specs=[whole] * 2,
            out_shape=[
                jax.ShapeDtypeStruct((tokens, part), jnp.float32),
                jax.ShapeDtypeStruct((tokens, 2 * LANES), jnp.bfloat16),
            ],
            compiler_params=params(16),
            cost_estimate=pl.CostEstimate(
                flops=16 * tokens * state_size * part, bytes_accessed=12 * tokens * part, transcendentals=0
            ),
            name="local_mixer",
        )(doc_start, decay, weight, values, query_rows, key_rows, *follow)

    rows = tokens // head_count
    direct = head_count == GROUPS
    me = jnp.reshape(head_index, (1,)).astype(jnp.int32)

    def gate_call(c, local, coefs, chain, earlier):
        joined = {apart: len(kept) for apart, kept in earlier.items()}
        if direct:
            out_shape = [
                jax.ShapeDtypeStruct((rows, part * (1 + joined.get(k, 0))), jnp.bfloat16)
                for k in range(head_count)
            ]
        else:
            out_shape = [jax.ShapeDtypeStruct((head_count, rows, part), jnp.bfloat16)]
        states = [one for got, _ in chain.arrived for one in got]
        if not four:
            states += [before for _, before in chain.arrived]
        arrivals = [len(got) for got, _ in chain.arrived]
        states += [one for apart in sorted(earlier) for one in earlier[apart]]
        return pl.pallas_call(
            functools.partial(
                gate_kernel,
                head_dim,
                heads,
                (near + 3) * heads,
                c * part,
                direct,
                far,
                four,
                arrivals,
                joined,
            ),
            in_specs=[smem] + [whole] * (4 + len(states)),
            out_specs=[whole] * len(out_shape),
            out_shape=out_shape,
            compiler_params=params(16),
            cost_estimate=pl.CostEstimate(
                flops=4 * tokens * state_size * part, bytes_accessed=8 * tokens * part, transcendentals=0
            ),
            name="far_and_gate",
        )(me, local, coefs, query_rows, gate_z, *states)

    def merge_call(bit, got, own, through, before, last):
        out_shape = [jax.ShapeDtypeStruct(got[0].shape, jnp.bfloat16)]
        if not last:
            out_shape += [
                jax.ShapeDtypeStruct(own.shape, jnp.float32),
                jax.ShapeDtypeStruct(through.shape, jnp.float32),
                jax.ShapeDtypeStruct(through.shape, jnp.float32),
            ]
        return pl.pallas_call(
            functools.partial(merge_kernel, bit, len(got)),
            in_specs=[whole] * (len(got) + 3),
            out_specs=[whole] * len(out_shape),
            out_shape=out_shape,
            compiler_params=params(4),
            cost_estimate=pl.CostEstimate(
                flops=8 * state_size * part, bytes_accessed=16 * state_size * part, transcendentals=0
            ),
            name="merge_blocks",
        )(*got, own, through, before)

    four = seq_count == 4
    if four:
        phases = [[[(0, 1)]], [[(1, 2), (2, 3)], [(1, 3)]]]
    else:
        phases = []
        for size in (2**bit for bit in range(far)):
            source = range(size - 1, seq_count, 2 * size)
            phases.append([[(s, s + up) for s in source] for up in range(1, size + 1)])

    class Chain:
        def __init__(self, c):
            self.own, self.moving, self.through = state_call(c)
            self.before = jnp.ones_like(self.through)
            self.arrived = []

        def post(self):
            got = [lax.ppermute(self.moving, "seq", p) for p in phases[len(self.arrived)]]
            self.arrived.append((got, self.before))

        def finish(self):
            while self.arrived and len(self.arrived) < far:
                got = self.arrived[-1][0]
                bit = len(self.arrived) - 1
                self.moving, *new = merge_call(
                    bit, got, self.own, self.through, self.before, four
                )
                if new:
                    self.own, self.through, self.before = new
                self.post()
            if four and len(self.arrived) == far:
                self.arrived = [([one], None) for got, _ in self.arrived for one in got]

    chains = [Chain(c) for c in range(chunks)]
    if far:
        for chain in chains:
            chain.post()
    for chain in chains:
        chain.finish()
    held = (1, 2)
    kept = {}
    pieces = []
    follow = [chains[-1].moving]
    for c in range(chunks):
        if c:
            follow = follow + [one for got, _ in chains[c].arrived for one in got]
        local, coefs = local_call(c, follow)
        final = c + 1 == chunks
        out = gate_call(c, local, coefs, chains[c], kept if final else {})
        follow = [out[0]]
        if direct:
            got = [out[0]] + [None] * (head_count - 1)
            for apart in partners(head_count, final):
                if not final and apart in held:
                    kept.setdefault(apart, []).append(out[apart])
                    continue
                pairs = [(source, source ^ apart) for source in range(head_count)]
                got[apart] = lax.ppermute(out[apart], "head", pairs)
            pieces.append(got)
        else:
            pieces.append(lax.all_to_all(out[0], "head", split_axis=0, concat_axis=0))

    gain = jnp.reshape(norm_gain, (1, -1))
    group_width = width * head_count // GROUPS

    if direct:
        operands, sources = [], []
        for k in range(head_count):
            mine = [got[k] for got in pieces if got[k] is not None]
            sources.append([(len(operands) + n, None) for n in range(len(mine))])
            operands += mine
    else:
        operands = pieces
        per_group = group_width // width
        sources = [
            [(c, g * per_group + n) for n in range(per_group) for c in range(chunks)]
            for g in range(GROUPS)
        ]
    return pl.pallas_call(
        functools.partial(norm_kernel, sources, direct),
        in_specs=[smem, whole] + [whole] * len(operands),
        out_specs=far_away,
        out_shape=jax.ShapeDtypeStruct((rows, width * head_count), jnp.bfloat16),
        scratch_shapes=[
            pltpu.VMEM((GROUPS, rows, group_width), jnp.bfloat16),
            pltpu.SemaphoreType.DMA((GROUPS,)),
        ],
        compiler_params=params(16),
        cost_estimate=pl.CostEstimate(
            flops=8 * tokens * width, bytes_accessed=4 * tokens * width, transcendentals=0
        ),
        name="norm_rows",
    )(me, gain, *operands)


def solution(mesh):
    in_specs = (
        P("seq", "head"),
        P("seq", "head"),
        P("seq", None, None),
        P("seq", None, None),
        P("seq", "head"),
        P("seq", "head", None),
        P(),
        P(),
    )
    out_specs = P(("seq", "head"), None)
    return jax.shard_map(body, mesh=mesh, in_specs=in_specs, out_specs=out_specs, check_vma=False)
```

```python
import functools

import jax
import jax.numpy as jnp
from jax import lax
from jax.experimental import pallas as pl
from jax.experimental.pallas import tpu as pltpu
from jax.sharding import PartitionSpec as P

MIXER_HEADS = 128
GROUPS = 8
SPAN = 64
TILE = 2 * SPAN
LANES = 128
WIDE = 2 * LANES
SUBLANES = 8
NEVER = -1e30
HIGHEST = lax.Precision.HIGHEST
MIB = 2**20


def dot(left, right, contract=((1,), (0,)), precision=None):
    return lax.dot_general(
        left, right, (contract, ((), ())), precision=precision, preferred_element_type=jnp.float32
    )


def iota(shape, axis):
    return lax.broadcasted_iota(jnp.int32, shape, axis)


def halves(coef):
    high = coef.astype(jnp.bfloat16)
    low = (coef - high.astype(jnp.float32)).astype(jnp.bfloat16)
    return jnp.concatenate([high, low], axis=1)


def spread(first, width, head_dim):
    row = jnp.bitwise_and(iota((2 * LANES, width), 0), LANES - 1)
    head = jnp.right_shift(iota((2 * LANES, width), 1), head_dim.bit_length() - 1)
    return jnp.where(row == head + first, 1.0, 0.0).astype(jnp.bfloat16)


def head_row(column, width, head_dim):
    shape = (column.shape[0], width)
    head = jnp.right_shift(iota(shape, 1), head_dim.bit_length() - 1)
    return jnp.sum(jnp.where(head == iota(shape, 0), column, 0.0), axis=0, keepdims=True)


def stack_rows(pieces):
    rows = sum(piece.shape[0] for piece in pieces)
    if rows < LANES:
        pieces = pieces + [jnp.zeros((LANES - rows, LANES), jnp.float32)]
    return jnp.transpose(jnp.concatenate(pieces, axis=0))


def tile_rows(decay):
    tiles = decay.shape[1] // TILE
    return jnp.concatenate([decay[:, b * TILE : (b + 1) * TILE] for b in range(tiles)], axis=0)


def resets(docs, tiles):
    first = lax.axis_index("seq") * (tiles * (TILE // SPAN))
    shut = [NEVER * docs[first + s].astype(jnp.float32) for s in range(tiles * (TILE // SPAN))]
    return [shut[2 * b : 2 * b + 2] for b in range(tiles)]


def pack(total, through):
    high = through.astype(jnp.bfloat16)
    low = (through - high.astype(jnp.float32)).astype(jnp.bfloat16)
    return jnp.concatenate([total.astype(jnp.bfloat16), high, low], axis=0)


def decay_kernel(head_dim, heads, docs, decay, *outs):
    chunks = len(outs) // 2
    tiles = decay.shape[1] // TILE
    shut = resets(docs, tiles)
    lane = iota((heads, TILE), 1)
    later = jnp.where(iota((TILE, TILE), 0) > iota((TILE, TILE), 1), 1.0, 0.0)
    for c in range(chunks):
        terms, through = outs[2 * c : 2 * c + 2]
        stacked = tile_rows(decay[c * heads : (c + 1) * heads, :])
        suffix = dot(stacked, later, precision=HIGHEST)
        totals = jnp.sum(stacked, axis=1, keepdims=True)
        after = jnp.zeros((heads, 1), jnp.float32)
        closed = jnp.float32(0.0)
        scales = [None] * tiles
        for b in reversed(range(tiles)):
            ends = jnp.where(lane < SPAN, closed + shut[b][1], closed)
            scales[b] = jnp.exp(suffix[b * heads : (b + 1) * heads] + after + ends)
            closed = closed + shut[b][1] + shut[b][0]
            after = after + totals[b * heads : (b + 1) * heads]
        terms[...] = halves(stack_rows(scales))
        row = head_row(jnp.exp(after + closed), through.shape[1], head_dim)
        through[...] = jnp.broadcast_to(row, through.shape)


def state_kernel(
    head_dim, heads, column, pieces, terms, through, keys, values, follow, state, message
):
    del follow
    width = state.shape[1]
    tokens = keys.shape[0]
    tiles = tokens // TILE
    rows = tokens // pieces
    owner = jnp.right_shift(
        jnp.bitwise_and(iota((1, 2 * LANES), 1), LANES - 1), heads.bit_length() - 1
    )
    shape = (2 * LANES, width)
    same = jnp.bitwise_and(iota(shape, 0), heads - 1) == jnp.right_shift(
        iota(shape, 1), head_dim.bit_length() - 1
    )
    one_hot = jnp.where(same, 1.0, 0.0).astype(jnp.bfloat16)
    chosen = [
        terms[...] * jnp.where(owner == b, 1.0, 0.0).astype(jnp.bfloat16) for b in range(tiles)
    ]
    total = jnp.zeros(state.shape, jnp.float32)
    for i in range(pieces):
        span = tiles // pieces
        here = slice(i * rows, (i + 1) * rows)
        scale = dot(jnp.concatenate(chosen[i * span : (i + 1) * span], axis=0), one_hot)
        scaled = values[here, column : column + width].astype(jnp.float32) * scale
        total += dot(keys[here, :], scaled.astype(jnp.bfloat16), ((0,), (0,)))
    state[...] = total
    message[...] = pack(total, through[...])


def merge_kernel(bit, arrivals, *refs):
    got, (own, through, before, message, *new) = refs[:arrivals], refs[arrivals:]
    states = own.shape[0]
    total = sum(part[...].astype(jnp.float32) for part in got)
    decays = total[states : states + SUBLANES] + total[states + SUBLANES :]
    upper = jnp.bitwise_and(jnp.right_shift(lax.axis_index("seq"), bit), 1).astype(jnp.float32)
    summed = own[...] + total[:states] * through[:1]
    passed = through[...] * (decays + (1.0 - upper))
    message[...] = pack(summed, passed)
    if new:
        new_own, new_through, new_before = new
        new_before[...] = before[...] * (decays + (1.0 - upper))
        new_own[...] = summed
        new_through[...] = passed


def local_kernel(
    head_dim, heads, chunk, far, docs, decay, weight, values, queries, keys, *rest
):
    out, coefs = rest[-2:]
    tokens, width = out.shape
    column = chunk * width
    mine = slice(chunk * heads, (chunk + 1) * heads)
    tiles = tokens // TILE
    near = tiles.bit_length() - 1
    shut = resets(docs, tiles)
    lane = iota((heads, TILE), 1)
    upto = jnp.where(iota((TILE, TILE), 0) <= iota((TILE, TILE), 1), 1.0, 0.0)
    all_sums = dot(tile_rows(decay[mine, :]), upto, precision=HIGHEST)
    causal = iota((TILE, TILE), 0) >= iota((TILE, TILE), 1)
    early = iota((SPAN, TILE), 1) < SPAN
    per_tile = LANES // head_dim
    lane_head = jnp.right_shift(iota((TILE, LANES), 1), head_dim.bit_length() - 1)
    hot = [spread((2 + i) * heads, width, head_dim) for i in range(near + 1)]

    def here(b):
        return slice(b * TILE, (b + 1) * TILE)

    columns, totals = [], []
    for b in range(tiles):
        sums = all_sums[b * heads : (b + 1) * heads]
        scale = [weight[level, mine, here(b)] for level in range(weight.shape[0])]
        last = jnp.broadcast_to(sums[:, TILE - 1 :], sums.shape)
        opened = sums + jnp.where(lane < SPAN, shut[b][0], shut[b][0] + shut[b][1])
        rows = [sums + jnp.log(scale[0]), sums + jnp.log(scale[1]) + shut[b][1]]
        for k in range(near):
            if (b >> k) & 1:
                since = sum(totals[(b >> k) << k : b], jnp.zeros_like(sums))
                rows.append(jnp.exp(opened + since) * scale[2 + k])
            else:
                rows.append(jnp.zeros_like(sums))
        rows.append(jnp.exp(last - sums + jnp.where(lane < SPAN, shut[b][1], 0.0)))
        since = sum(totals, jnp.zeros_like(sums))
        rows += [jnp.exp(opened + since) * scale[2 + near + m] for m in range(far)]
        totals.append(last + (shut[b][0] + shut[b][1]))
        columns.append(stack_rows(rows))
        coefs[here(b), :] = halves(columns[b])

    whole = (tiles - 1) * TILE
    slots = {}
    if tiles > 1:
        scaled = values[:whole, column : column + width].astype(jnp.float32)
        scaled = (scaled * dot(coefs[:whole, :], hot[near])).astype(jnp.bfloat16)
    held = [None] * near
    for b in range(tiles - 1):
        now = dot(keys[here(b), :], scaled[here(b), :], ((0,), (0,)))
        for k in range(near):
            if not (b >> k) & 1:
                held[k] = now
                slots[k, b >> k] = now.astype(jnp.bfloat16)
                break
            since = sum(totals[(b >> k) << k : b + 1])
            now = now + held[k] * head_row(jnp.exp(since)[:, :1], width, head_dim)

    for b in range(tiles):
        sums = all_sums[b * heads : (b + 1) * heads]
        scores = dot(queries[here(b), :], keys[here(b), :], ((1,), (1,)))
        scores = jnp.where(causal, scores, 0.0)
        block = values[here(b), column : column + width]
        mixed = []
        for part in range(width // LANES):
            values_here = block[:, part * LANES : (part + 1) * LANES]
            left, right = [], []
            for inner in range(per_tile):
                head = part * per_tile + inner
                own = jnp.broadcast_to(columns[b][:, head : head + 1], (TILE, TILE))
                beside = columns[b][SPAN:, heads + head : heads + head + 1]
                below = jnp.where(early, jnp.broadcast_to(beside, (SPAN, TILE)), own[SPAN:])
                gap = jnp.concatenate([own[:SPAN], below], axis=0) - sums[head : head + 1, :]
                left.append((jnp.exp(jnp.minimum(gap, 80.0)) * scores).astype(jnp.bfloat16))
                right.append(jnp.where(lane_head == inner, values_here, jnp.zeros_like(values_here)))
            mixed.append(dot(jnp.concatenate(left, axis=1), jnp.concatenate(right, axis=0)))
        for at in range(0, width, WIDE):
            lanes = slice(at, min(at + WIDE, width))
            total = jnp.concatenate(mixed[at // LANES : (at + WIDE) // LANES], axis=1)
            for k in range(near):
                if (b >> k) & 1:
                    reached = dot(queries[here(b), :], slots[k, (b >> k) - 1][:, lanes])
                    total += dot(coefs[here(b), :], hot[k][:, lanes]) * reached
            out[here(b), lanes] = total


def gate_kernel(
    head_dim, heads, first, column, xor, far, four, arrivals, joined, me, *refs
):
    local, coefs, queries, gate, *rest = refs
    got = [rest[sum(arrivals[:m]) : sum(arrivals[: m + 1])] for m in range(len(arrivals))]
    at = sum(arrivals)
    befores = 0 if four else far
    before, rest = rest[at : at + befores], rest[at + befores :]
    earlier, outs = rest[: sum(joined.values())], rest[sum(joined.values()) :]
    count = len(outs) if xor else outs[0].shape[0]
    rows = local.shape[0] // count
    width = local.shape[1]
    states = queries.shape[1]
    hot = [spread(first + m * heads, width, head_dim) for m in range(far)]
    arrived = []
    if four:
        near_by, next_by, over = (part[...].astype(jnp.float32) for (part,) in got)
        decays = next_by[states : states + SUBLANES] + next_by[states + SUBLANES :]
        last = jnp.where(lax.axis_index("seq") == 3, 1.0, 0.0)
        arrived.append(near_by[:states] + next_by[:states] * last)
        arrived.append(next_by[:states] * (1.0 - last) + over[:states] * decays[:1])
        arrived = [state.astype(jnp.bfloat16) for state in arrived]
    else:
        for m in range(far):
            state = sum(part[:states, :].astype(jnp.float32) for part in got[m])
            arrived.append((state * before[m][:1]).astype(jnp.bfloat16))

    def fill(place, out):
        here = pl.ds(pl.multiple_of(place * rows, rows), rows)
        for at in range(0, width, WIDE):
            end = min(at + WIDE, width)
            total = local[here, at:end]
            for m in range(far):
                reached = dot(queries[here, :], arrived[m][:, at:end])
                total += dot(coefs[here, :], hot[m][:, at:end]) * reached
            opened = 0.5 * gate[here, column + at : column + end].astype(jnp.float32)
            out[:, at:end] = (total * opened * (1.0 + jnp.tanh(opened))).astype(jnp.bfloat16)

    if xor:
        at = 0
        for index, out in enumerate(outs):
            prior = joined.get(index, 0) * width
            for start in range(0, prior, width):
                out[:, start : start + width] = earlier[at][...]
                at += 1
            fill(jnp.bitwise_xor(me[0], index), out.at[:, prior : prior + width])
    else:

        @pl.loop(0, count)
        def _(index):
            fill(index, outs[0].at[index])


def norm_kernel(sources, xor, me, gain, *rest):
    parts, (out, done, sent) = rest[:-3], rest[-3:]
    rows, group_width = done.shape[1:]
    some = min(rows, 4 * SUBLANES)
    copies = []
    for index, places in enumerate(sources):
        group = jnp.bitwise_xor(me[0], index) if xor else index
        columns = pl.ds(pl.multiple_of(group * group_width, group_width), group_width)
        for top in range(0, rows, some):
            here = slice(top, top + some)
            blocks = [parts[n][here, :] if at is None else parts[n][at, here, :] for n, at in places]
            blocks = [block.astype(jnp.float32) for block in blocks]
            square = sum(jnp.sum(block * block, axis=1, keepdims=True) for block in blocks)
            scale = lax.rsqrt(square / group_width + 1e-05)
            normed = jnp.concatenate([block * scale for block in blocks], axis=1)
            done[index, here, :] = (normed * gain[:, columns]).astype(out.dtype)
        copies.append(pltpu.make_async_copy(done.at[index], out.at[:, columns], sent.at[index]))
        copies[-1].start()
    for copy in copies:
        copy.wait()


def partners(count, final):
    if final:
        return sorted(range(1, count), key=lambda apart: (apart in (1, 4), apart != 5, -apart))
    return sorted(range(1, count), key=lambda apart: (-apart.bit_count(), -apart))


def params(limit):
    return pltpu.CompilerParams(vmem_limit_bytes=limit * MIB)


def body(values, gate_z, b_keys, c_queries, log_decay, level_weight, doc_start, norm_gain):
    tokens, width = values.shape
    heads_here = log_decay.shape[1]
    head_dim = width // heads_here
    state_size = b_keys.shape[2]
    tiles = tokens // TILE
    near = tiles.bit_length() - 1
    seq_count = lax.axis_size("seq")
    far = seq_count.bit_length() - 1
    head_count = lax.axis_size("head")
    head_index = lax.axis_index("head")
    group_index = head_index * heads_here // (MIXER_HEADS // GROUPS)
    decay = jnp.transpose(log_decay)
    weight = jnp.transpose(level_weight, (2, 1, 0))
    heads = SUBLANES
    if heads_here < heads:
        short = heads - heads_here
        decay = jnp.pad(decay, ((0, short), (0, 0)))
        weight = jnp.pad(weight, ((0, 0), (0, short), (0, 0)), constant_values=1.0)
    chunks = max(1, heads_here // heads)
    part = width // chunks
    levels = weight.shape[0]
    smem = pl.BlockSpec(memory_space=pltpu.SMEM)
    parts = [values[:, :part]] + [values] * (chunks - 1)

    whole = pl.BlockSpec(memory_space=pltpu.VMEM)
    anywhere = pl.BlockSpec(memory_space=pl.ANY)
    far_away = pl.BlockSpec(memory_space=pltpu.HBM)

    decays = pl.pallas_call(
        functools.partial(decay_kernel, head_dim, heads),
        in_specs=[smem, whole],
        out_specs=[whole] * (2 * chunks),
        out_shape=[
            jax.ShapeDtypeStruct((LANES, 2 * LANES), jnp.bfloat16),
            jax.ShapeDtypeStruct((SUBLANES, part), jnp.float32),
        ]
        * chunks,
        compiler_params=params(8),
        cost_estimate=pl.CostEstimate(
            flops=tokens * width, bytes_accessed=4 * tokens * part, transcendentals=0
        ),
        name="token_decays",
    )(doc_start, decay)

    group_index, _ = lax.optimization_barrier((group_index, decays[1]))
    key_rows = lax.dynamic_index_in_dim(b_keys, group_index, 1, keepdims=False)
    query_rows = lax.dynamic_index_in_dim(c_queries, group_index, 1, keepdims=False)

    def state_call(c):
        terms, through = decays[2 * c : 2 * c + 2]
        pieces = min(4, tiles)
        state, message = pl.pallas_call(
            functools.partial(state_kernel, head_dim, heads, c * part, pieces),
            in_specs=[whole, whole, whole, whole, anywhere],
            out_specs=[whole, whole],
            out_shape=[
                jax.ShapeDtypeStruct((state_size, part), jnp.float32),
                jax.ShapeDtypeStruct((state_size + 2 * SUBLANES, part), jnp.bfloat16),
            ],
            compiler_params=params(16),
            cost_estimate=pl.CostEstimate(
                flops=4 * tokens * state_size * part, bytes_accessed=3 * tokens * part, transcendentals=0
            ),
            name="block_state",
        )(terms, through, key_rows, parts[c], key_rows if c == 0 else query_rows)
        return state, message, through

    def local_call(c, follow):
        return pl.pallas_call(
            functools.partial(local_kernel, head_dim, heads, c, far),
            in_specs=[smem] + [whole] * 5 + [anywhere] * len(follow),
            out_specs=[whole] * 2,
            out_shape=[
                jax.ShapeDtypeStruct((tokens, part), jnp.float32),
                jax.ShapeDtypeStruct((tokens, 2 * LANES), jnp.bfloat16),
            ],
            compiler_params=params(16),
            cost_estimate=pl.CostEstimate(
                flops=16 * tokens * state_size * part, bytes_accessed=12 * tokens * part, transcendentals=0
            ),
            name="local_mixer",
        )(doc_start, decay, weight, values, query_rows, key_rows, *follow)

    rows = tokens // head_count
    direct = head_count == GROUPS
    me = jnp.reshape(head_index, (1,)).astype(jnp.int32)

    def gate_call(c, local, coefs, chain, earlier):
        joined = {apart: len(kept) for apart, kept in earlier.items()}
        if direct:
            out_shape = [
                jax.ShapeDtypeStruct((rows, part * (1 + joined.get(k, 0))), jnp.bfloat16)
                for k in range(head_count)
            ]
        else:
            out_shape = [jax.ShapeDtypeStruct((head_count, rows, part), jnp.bfloat16)]
        states = [one for got, _ in chain.arrived for one in got]
        if not four:
            states += [before for _, before in chain.arrived]
        arrivals = [len(got) for got, _ in chain.arrived]
        states += [one for apart in sorted(earlier) for one in earlier[apart]]
        return pl.pallas_call(
            functools.partial(
                gate_kernel,
                head_dim,
                heads,
                (near + 3) * heads,
                c * part,
                direct,
                far,
                four,
                arrivals,
                joined,
            ),
            in_specs=[smem] + [whole] * (4 + len(states)),
            out_specs=[whole] * len(out_shape),
            out_shape=out_shape,
            compiler_params=params(16),
            cost_estimate=pl.CostEstimate(
                flops=4 * tokens * state_size * part, bytes_accessed=8 * tokens * part, transcendentals=0
            ),
            name="far_and_gate",
        )(me, local, coefs, query_rows, gate_z, *states)

    def merge_call(bit, got, own, through, before, last):
        out_shape = [jax.ShapeDtypeStruct(got[0].shape, jnp.bfloat16)]
        if not last:
            out_shape += [
                jax.ShapeDtypeStruct(own.shape, jnp.float32),
                jax.ShapeDtypeStruct(through.shape, jnp.float32),
                jax.ShapeDtypeStruct(through.shape, jnp.float32),
            ]
        return pl.pallas_call(
            functools.partial(merge_kernel, bit, len(got)),
            in_specs=[whole] * (len(got) + 3),
            out_specs=[whole] * len(out_shape),
            out_shape=out_shape,
            compiler_params=params(4),
            cost_estimate=pl.CostEstimate(
                flops=8 * state_size * part, bytes_accessed=16 * state_size * part, transcendentals=0
            ),
            name="merge_blocks",
        )(*got, own, through, before)

    four = seq_count == 4
    if four:
        phases = [[[(0, 1)]], [[(1, 2), (2, 3)], [(1, 3)]]]
    else:
        phases = []
        for size in (2**bit for bit in range(far)):
            source = range(size - 1, seq_count, 2 * size)
            phases.append([[(s, s + up) for s in source] for up in range(1, size + 1)])

    class Chain:
        def __init__(self, c):
            self.own, self.moving, self.through = state_call(c)
            self.before = jnp.ones_like(self.through)
            self.arrived = []

        def post(self):
            got = [lax.ppermute(self.moving, "seq", p) for p in phases[len(self.arrived)]]
            self.arrived.append((got, self.before))

        def finish(self):
            while self.arrived and len(self.arrived) < far:
                got = self.arrived[-1][0]
                bit = len(self.arrived) - 1
                self.moving, *new = merge_call(
                    bit, got, self.own, self.through, self.before, four
                )
                if new:
                    self.own, self.through, self.before = new
                self.post()
            if four and len(self.arrived) == far:
                self.arrived = [([one], None) for got, _ in self.arrived for one in got]

    chains = [Chain(c) for c in range(chunks)]
    if far:
        for chain in chains:
            chain.post()
    for chain in chains:
        chain.finish()
    held = (1, 2)
    kept = {}
    pieces = []
    follow = [chains[-1].moving]
    for c in range(chunks):
        if c:
            follow = follow + [one for got, _ in chains[c].arrived for one in got]
        local, coefs = local_call(c, follow)
        final = c + 1 == chunks
        out = gate_call(c, local, coefs, chains[c], kept if final else {})
        follow = [out[0]]
        if direct:
            got = [out[0]] + [None] * (head_count - 1)
            for apart in partners(head_count, final):
                if not final and apart in held:
                    kept.setdefault(apart, []).append(out[apart])
                    continue
                pairs = [(source, source ^ apart) for source in range(head_count)]
                got[apart] = lax.ppermute(out[apart], "head", pairs)
            pieces.append(got)
        else:
            pieces.append(lax.all_to_all(out[0], "head", split_axis=0, concat_axis=0))

    gain = jnp.reshape(norm_gain, (1, -1))
    group_width = width * head_count // GROUPS

    if direct:
        operands, sources = [], []
        for k in range(head_count):
            mine = [got[k] for got in pieces if got[k] is not None]
            sources.append([(len(operands) + n, None) for n in range(len(mine))])
            operands += mine
    else:
        operands = pieces
        per_group = group_width // width
        sources = [
            [(c, g * per_group + n) for n in range(per_group) for c in range(chunks)]
            for g in range(GROUPS)
        ]
    return pl.pallas_call(
        functools.partial(norm_kernel, sources, direct),
        in_specs=[smem, whole] + [whole] * len(operands),
        out_specs=far_away,
        out_shape=jax.ShapeDtypeStruct((rows, width * head_count), jnp.bfloat16),
        scratch_shapes=[
            pltpu.VMEM((GROUPS, rows, group_width), jnp.bfloat16),
            pltpu.SemaphoreType.DMA((GROUPS,)),
        ],
        compiler_params=params(16),
        cost_estimate=pl.CostEstimate(
            flops=8 * tokens * width, bytes_accessed=4 * tokens * width, transcendentals=0
        ),
        name="norm_rows",
    )(me, gain, *operands)


def solution(mesh):
    in_specs = (
        P("seq", "head"),
        P("seq", "head"),
        P("seq", None, None),
        P("seq", None, None),
        P("seq", "head"),
        P("seq", "head", None),
        P(),
        P(),
    )
    out_specs = P(("seq", "head"), None)
    return jax.shard_map(body, mesh=mesh, in_specs=in_specs, out_specs=out_specs, check_vma=False)
```
